256 devices in a mesh: lon: 32 (over y_lo, z, core), lev: 8 (over x, y_hi).
Axes of the slice: x: 4, y: 4 (y_hi: 2, y_lo: 2; y = y_hi * 2 + y_lo), z: 8, core: 2. Of those that a mesh axis runs over, the one named last changes fastest.
Arguments:
- query_level: bfloat16 [8, 32, 128, 1024], P('lev', None, 'lon'), may hold values from -45 to 45
- key_level: bfloat16 [8, 32, 128, 1024], P('lev', None, 'lon'), may hold values from -15 to 15
- value_level: bfloat16 [8, 32, 128, 1024], P('lev', None, 'lon'), may hold values from -6 to 6
- block_lists: int32 [32, 4, 15], P('lon'), may hold values from 0 to 23, as said below
- query_column: bfloat16 [8, 32, 128, 1024], P(None, 'lev', 'lon'), may hold values from -45 to 45
- key_column: bfloat16 [8, 32, 128, 1024], P(None, 'lev', 'lon'), may hold values from -15 to 15
- grad_output: bfloat16 [8, 32, 128, 1024], P(None, 'lev', 'lon'), may hold values from -6 to 6
Outputs:
- grad_query_level: bfloat16 [8, 32, 128, 1024], P('lev', None, 'lon')
- grad_key_level: bfloat16 [8, 32, 128, 1024], P('lev', None, 'lon')
- grad_value_level: bfloat16 [8, 32, 128, 1024], P('lev', None, 'lon')
- grad_query_column: bfloat16 [8, 32, 128, 1024], P(None, 'lev', 'lon')
- grad_key_column: bfloat16 [8, 32, 128, 1024], P(None, 'lev', 'lon')
The draws below stay inside these ranges and needn't reach their ends.
Inputs may be any that keep to these rules, and one draw needn't show every extreme that they name: `block_lists`: the entries of one row are distinct key blocks of the tile's extended region, and every row lists the two key blocks that lie under its own query block.
All inputs are finite; a program needn't handle non-finite values.
Results may differ from the reference program's by a relative error of at most 0.0072.
Values may be sent and summed in bfloat16 or wider, within the bound.
No kernel may reach another device: no remote copies, remote signals or barrier semaphores. Data moves between devices by JAX's collectives and lax.ppermute only.
A program may use at most 64 MiB of HBM per device.

```python
import math
import jax
import jax.numpy as jnp
from jax import lax

D = 1024
HEADS = 16
LAT = 32
LON_DEV = 4
HALO = 4
LEVELS = 8
LON = 128
TILES = 32
QBN = 4
KBN = 24
NBR = 15
N_LON = 32


def draw_query_level(key, part):
    key = jax.random.fold_in(key, 11)
    shape = (LEVELS, LAT, LON, D)
    return jnp.clip(jax.random.normal(key, shape, jnp.float32), -5.0, 5.0).astype(jnp.bfloat16)


def draw_key_level(key, part):
    key = jax.random.fold_in(key, 12)
    shape = (LEVELS, LAT, LON, D)
    return jnp.clip(jax.random.normal(key, shape, jnp.float32), -5.0, 5.0).astype(jnp.bfloat16)


def draw_query_column(key, part):
    key = jax.random.fold_in(key, 13)
    shape = (LEVELS, LAT, LON, D)
    return jnp.clip(jax.random.normal(key, shape, jnp.float32), -5.0, 5.0).astype(jnp.bfloat16)


def draw_key_column(key, part):
    key = jax.random.fold_in(key, 14)
    shape = (LEVELS, LAT, LON, D)
    return jnp.clip(jax.random.normal(key, shape, jnp.float32), -5.0, 5.0).astype(jnp.bfloat16)


def draw_block_lists(key, part):
    key = jax.random.fold_in(key, 7)
    split_keys = jax.random.split(key, TILES * QBN)
    shuffled = jax.vmap(lambda one_key: jax.random.permutation(one_key, KBN))(split_keys)
    shuffled = shuffled.reshape(TILES, QBN, KBN).astype(jnp.int32)
    query_ids = jnp.arange(QBN, dtype=jnp.int32)
    lat_block = query_ids // (LON_DEV // 4)
    col_block = query_ids % (LON_DEV // 4)
    first_block = lat_block * ((LON_DEV + 2 * HALO) // 2) + (HALO + 4 * col_block) // 2
    block_ids = jnp.arange(KBN, dtype=jnp.int32)
    own_blocks = jnp.logical_or(block_ids[None, :] == first_block[:, None], block_ids[None, :] == first_block[:, None] + 1)
    priority = jnp.where(own_blocks[None, :, :], shuffled - KBN, shuffled)
    ranked = jnp.argsort(priority, axis=-1)
    return ranked[:, :, :NBR].astype(jnp.int32)


def block_levels(own_key, shape, cuts, low, largest):
    def one(axis_at, blocks):
        draws = jax.random.uniform(jax.random.fold_in(jax.random.fold_in(own_key, 6), axis_at), (blocks,), jnp.float32, low / len(cuts), largest / len(cuts))
        return jnp.repeat(jnp.exp(draws), shape[axis_at] // blocks).reshape((-1,) + (1,) * (len(shape) - axis_at - 1))

    loudness = one(*cuts[0])
    for cut in cuts[1:]:
        loudness = loudness * one(*cut)
    return loudness


def scatter_about(stream_key, shape, deviation, reach, cuts=(), held_as=jnp.bfloat16):
    values = jax.random.normal(stream_key, shape, jnp.float32) * deviation
    if len(cuts) > 0:
        values = block_levels(stream_key, shape, cuts, -0.22, 0.18) * values
    return jnp.clip(values, min=-reach, max=reach).astype(held_as)


def setup_inputs(seed: int = 0) -> dict:
    keys = jax.random.split(jax.random.key(seed), 8)
    return {
        "query_level": draw_query_level(jax.random.fold_in(keys[7], 71), 0),
        "key_level": draw_key_level(jax.random.fold_in(keys[7], 71), 0),
        "value_level": scatter_about(keys[2], (LEVELS, LAT, LON, D), 1.0, 6.0, ((0, 8), (2, 32))),
        "block_lists": draw_block_lists(jax.random.fold_in(keys[7], 71), 0),
        "query_column": draw_query_column(jax.random.fold_in(keys[7], 71), 0),
        "key_column": draw_key_column(jax.random.fold_in(keys[7], 71), 0),
        "grad_output": scatter_about(keys[6], (LEVELS, LAT, LON, D), 1.0, 6.0, ((1, 8), (2, 32))),
    }


NEGATIVE = -1e+30

def token_mask(list_rows, lat_rows, lon_dev, extent):
    key_blocks = lat_rows // 8 * (extent // 2)
    block_ids = jnp.arange(key_blocks, dtype=jnp.int32)
    listed = jnp.any(list_rows[:, :, None] == block_ids[None, None, :], axis=1)
    listed = listed.reshape(lat_rows // 8, lon_dev // 4, lat_rows // 8, extent // 2)
    spread = jnp.broadcast_to(listed[:, None, :, None, :, None, :, None], (lat_rows // 8, 8, lon_dev // 4, 4, lat_rows // 8, 8, extent // 2, 2))
    return spread.reshape(lat_rows * lon_dev, lat_rows * extent)

def masked_softmax(scores, allowed):
    scores = jnp.where(allowed, scores, NEGATIVE)
    row_max = lax.optimization_barrier(jnp.max(scores, axis=-1, keepdims=True))
    raised = jnp.exp(scores - row_max)
    return raised / lax.optimization_barrier(jnp.sum(raised, axis=-1, keepdims=True))

def plain_softmax(scores):
    row_max = lax.optimization_barrier(jnp.max(scores, axis=-1, keepdims=True))
    raised = jnp.exp(scores - row_max)
    return raised / lax.optimization_barrier(jnp.sum(raised, axis=-1, keepdims=True))

def rounded_rim(part):
    return lax.optimization_barrier(part.astype(jnp.bfloat16)).astype(jnp.float32)

def reference(query_level, key_level, value_level, block_lists, query_column, key_column, grad_output):
    head_dim = D // HEADS
    scaling = 1.0 / math.sqrt(head_dim)
    extent = LON_DEV + 2 * HALO
    tile_count = N_LON
    tile_masks = jax.vmap(lambda rows_list: token_mask(rows_list, LAT, LON_DEV, extent))(block_lists)

    def extend(plane):
        padded = jnp.concatenate([plane[:, LON - HALO:], plane, plane[:, :HALO]], axis=1)
        starts = jnp.arange(tile_count, dtype=jnp.int32) * LON_DEV
        return lax.map(lambda start: lax.dynamic_slice_in_dim(padded, start, extent, 1), starts)

    def tile_view(plane):
        tiled = plane.reshape(LAT, tile_count, LON_DEV, D).transpose(1, 0, 2, 3)
        return tiled.reshape(tile_count, LAT * LON_DEV, HEADS, head_dim)

    def plane_view(tiled):
        return tiled.reshape(tile_count, LAT, LON_DEV, D).transpose(1, 0, 2, 3).reshape(LAT, LON, D)

    def tile_probs(query_tile, key_tile, allowed):
        key_flat = key_tile.reshape(LAT * extent, HEADS, head_dim).astype(jnp.float32)
        scores = jnp.einsum('qhd,khd->hqk', query_tile.astype(jnp.float32), key_flat) * scaling
        return masked_softmax(scores, allowed)

    def forward_level(bundle):
        query_plane, key_plane, value_plane = bundle
        key_ext = extend(key_plane)
        value_ext = extend(value_plane)
        query_tiles = tile_view(query_plane)

        def one_tile(tile_bundle):
            query_tile, key_tile, value_tile, allowed = tile_bundle
            attn_probs = tile_probs(query_tile, key_tile, allowed)
            value_flat = value_tile.reshape(LAT * extent, HEADS, head_dim).astype(jnp.float32)
            probs_b = attn_probs.astype(jnp.bfloat16).astype(jnp.float32)
            return jnp.einsum('hqk,khd->qhd', probs_b, value_flat).astype(jnp.bfloat16)
        attended_tiles = lax.map(one_tile, (query_tiles, key_ext, value_ext, tile_masks))
        return plane_view(attended_tiles)
    attended = lax.map(forward_level, (query_level, key_level, value_level))

    def column_row(bundle):
        col_query, col_key, col_grad, col_att = bundle

        def heads_view(array):
            return array.reshape(LEVELS, LON, HEADS, head_dim).astype(jnp.float32)
        column_query = heads_view(col_query)
        column_key = heads_view(col_key)
        column_grad = heads_view(col_grad)
        column_att = heads_view(col_att)
        col_probs = plain_softmax(jnp.einsum('lthd,mthd->thlm', column_query, column_key) * scaling)
        d_col_probs = jnp.einsum('lthd,mthd->thlm', column_grad, column_att)
        d_col_scores = col_probs * (d_col_probs - lax.optimization_barrier(jnp.sum(col_probs * d_col_probs, axis=-1, keepdims=True)))
        scores_b = d_col_scores.astype(jnp.bfloat16).astype(jnp.float32)
        probs_b = col_probs.astype(jnp.bfloat16).astype(jnp.float32)
        grad_query = (jnp.einsum('thlm,mthd->lthd', scores_b, column_key) * scaling).astype(jnp.bfloat16)
        grad_key = (jnp.einsum('thlm,lthd->mthd', scores_b, column_query) * scaling).astype(jnp.bfloat16)
        grad_att = jnp.einsum('thlm,lthd->mthd', probs_b, column_grad).astype(jnp.bfloat16)
        return (grad_query.reshape(LEVELS, LON, D), grad_key.reshape(LEVELS, LON, D), grad_att.reshape(LEVELS, LON, D))
    rows_first = tuple((jnp.moveaxis(array, 1, 0) for array in (query_column, key_column, grad_output, attended)))
    grad_qc_rows, grad_kc_rows, grad_att_rows = lax.map(column_row, rows_first)
    grad_query_column = jnp.moveaxis(grad_qc_rows, 0, 1)
    grad_key_column = jnp.moveaxis(grad_kc_rows, 0, 1)
    grad_attended = jnp.moveaxis(grad_att_rows, 0, 1)

    def assemble(terms):
        interior = terms[:, :, HALO:HALO + LON_DEV]
        left_part = rounded_rim(terms[:, :, :HALO])
        right_part = rounded_rim(terms[:, :, HALO + LON_DEV:])
        left_rim = jnp.pad(left_part, ((0, 0), (0, 0), (LON_DEV - HALO, 0), (0, 0)))
        right_rim = jnp.pad(right_part, ((0, 0), (0, 0), (0, LON_DEV - HALO), (0, 0)))
        summed = interior + jnp.roll(left_rim, -1, axis=0) + jnp.roll(right_rim, 1, axis=0)
        return summed.transpose(1, 0, 2, 3).reshape(LAT, LON, D).astype(jnp.bfloat16)

    def backward_level(bundle):
        query_plane, key_plane, value_plane, grad_plane = bundle
        key_ext = extend(key_plane)
        value_ext = extend(value_plane)
        query_tiles = tile_view(query_plane)
        grad_tiles = tile_view(grad_plane)

        def one_tile(tile_bundle):
            query_tile, key_tile, value_tile, grad_tile, allowed = tile_bundle
            attn_probs = tile_probs(query_tile, key_tile, allowed)
            probs_b = attn_probs.astype(jnp.bfloat16).astype(jnp.float32)
            key_flat = key_tile.reshape(LAT * extent, HEADS, head_dim).astype(jnp.float32)
            value_flat = value_tile.reshape(LAT * extent, HEADS, head_dim).astype(jnp.float32)
            grad_att = grad_tile.astype(jnp.float32)
            query_flat = query_tile.astype(jnp.float32)
            d_probs = jnp.einsum('qhd,khd->hqk', grad_att, value_flat)
            d_scores = attn_probs * (d_probs - lax.optimization_barrier(jnp.sum(attn_probs * d_probs, axis=-1, keepdims=True)))
            scores_b = d_scores.astype(jnp.bfloat16).astype(jnp.float32)
            grad_query = (jnp.einsum('hqk,khd->qhd', scores_b, key_flat) * scaling).astype(jnp.bfloat16)
            key_terms = jnp.einsum('hqk,qhd->khd', scores_b, query_flat) * scaling
            value_terms = jnp.einsum('hqk,qhd->khd', probs_b, grad_att)
            return (grad_query, key_terms.reshape(LAT, extent, D), value_terms.reshape(LAT, extent, D))
        grad_query_tiles, key_terms, value_terms = lax.map(one_tile, (query_tiles, key_ext, value_ext, grad_tiles, tile_masks))
        return (plane_view(grad_query_tiles), assemble(key_terms), assemble(value_terms))
    grad_query_level, grad_key_level, grad_value_level = lax.map(backward_level, (query_level, key_level, value_level, grad_attended))
    return (grad_query_level, grad_key_level, grad_value_level, grad_query_column, grad_key_column)
```

```python
import functools
import math

import jax
import jax.numpy as jnp
from jax import lax
from jax.experimental import pallas as pl
from jax.experimental.pallas import tpu as pltpu
from jax.sharding import PartitionSpec as P

HEADS = 16
HALO = 4
ROWS = 128
PAIR = 128
NEGATIVE = -1e30
F32 = jnp.float32
BF16 = jnp.bfloat16

VMEM = pl.BlockSpec(memory_space=pltpu.VMEM)
SMEM = pl.BlockSpec(memory_space=pltpu.SMEM)


def tokens(ref, pair):
    return ref[:, :, :, pl.ds(pair * PAIR, PAIR)].reshape(ROWS, PAIR)


def put(ref, pair, value):
    shape = ref.shape[:-1] + (PAIR,)
    ref[:, :, :, pl.ds(pair * PAIR, PAIR)] = value.astype(ref.dtype).reshape(shape)


def both_heads(block):
    lane = lax.broadcasted_iota(jnp.int32, (1, PAIR), 1)
    first = (lane < PAIR // 2).astype(F32).astype(BF16)
    second = (lane >= PAIR // 2).astype(F32).astype(BF16)
    return jnp.concatenate([block * first, block * second], axis=0)


def outer(a, b):
    return lax.dot_general(a, b, (((1,), (1,)), ((), ())), preferred_element_type=F32)


def inner(a, b):
    return lax.dot_general(a, b, (((1,), (0,)), ((), ())), preferred_element_type=F32)


def own_features(both):
    half = PAIR // 2
    return jnp.concatenate([both[:half, :ROWS], both[half:, ROWS:]], axis=0)


def softmax_over_rows(scores):
    top = jnp.max(scores, axis=0, keepdims=True)
    raised = jnp.exp(scores - top)
    return raised * (1.0 / jnp.sum(raised, axis=0, keepdims=True))


def score_grads(probs, d_probs):
    return probs * (d_probs - jnp.sum(probs * d_probs, axis=0, keepdims=True))


def column_bias():
    key = lax.broadcasted_iota(jnp.int32, (ROWS, 2 * ROWS), 0)
    query = lax.broadcasted_iota(jnp.int32, (ROWS, 2 * ROWS), 1)
    return jnp.where((key & 15) == (query & 15), 0.0, NEGATIVE).astype(F32)


def column_forward(q_ref, k_ref, g_ref, out_ref):
    bias = column_bias()
    for pair in range(HEADS // 2):
        queries = both_heads(tokens(q_ref, pair) * BF16(0.125))
        probs = softmax_over_rows(outer(tokens(k_ref, pair), queries) + bias)
        put(out_ref, pair, inner(probs.astype(BF16), both_heads(tokens(g_ref, pair))))


def column_backward(q_ref, k_ref, g_ref, a_ref, dq_ref, dk_ref):
    bias = column_bias()
    for pair in range(HEADS // 2):
        queries = both_heads(tokens(q_ref, pair) * BF16(0.125))
        keys = tokens(k_ref, pair)
        probs = softmax_over_rows(outer(keys, queries) + bias)
        d_probs = outer(tokens(a_ref, pair), both_heads(tokens(g_ref, pair)))
        d_scores = score_grads(probs, d_probs).astype(BF16)
        put(dk_ref, pair, inner(d_scores, queries))
        grad_query = own_features(inner(keys.T, d_scores)) * 0.125
        put(dq_ref, pair, grad_query.astype(BF16).T)


def level_bias(lists_ref):
    lane = lax.broadcasted_iota(jnp.int32, (1, ROWS), 1)
    listed = jnp.zeros((1, ROWS), jnp.int32)
    for block in range(4):
        bits = jnp.int32(0)
        for j in range(15):
            bits = bits | lax.shift_left(jnp.int32(1), lists_ref[0, block, j])
        listed = jnp.where(lane // 32 == block, bits, listed)
    row = lax.broadcasted_iota(jnp.int32, (3 * ROWS, ROWS), 0)
    part = row // ROWS
    lat = (row % ROWS) // 4
    column = row % 4
    key_block = (lat // 8) * 6 + part * 2 + column // 2
    allowed = lax.shift_right_logical(jnp.broadcast_to(listed, row.shape), key_block) & 1
    return jnp.where(allowed == 1, 0.0, NEGATIVE).astype(F32)


def level_kernel(
    lists_ref, q_ref, k_ref, v_ref, kl_ref, vl_ref, kr_ref, vr_ref, g_ref,
    att_ref, dq_ref, dk_ref, dv_ref, dkl_ref, dvl_ref, dkr_ref, dvr_ref,
):
    bias = level_bias(lists_ref)
    bias = jnp.concatenate([bias, bias], axis=1)
    for pair in range(HEADS // 2):
        queries = both_heads(tokens(q_ref, pair) * BF16(0.125))
        grads = both_heads(tokens(g_ref, pair))
        keys = jnp.concatenate([tokens(r, pair) for r in (kl_ref, k_ref, kr_ref)], axis=0)
        values = jnp.concatenate([tokens(r, pair) for r in (vl_ref, v_ref, vr_ref)], axis=0)
        probs = softmax_over_rows(outer(keys, queries) + bias)
        probs_b = probs.astype(BF16)
        attended = own_features(inner(values.T, probs_b))
        put(att_ref, pair, attended.astype(BF16).T)
        d_scores = score_grads(probs, outer(values, grads)).astype(BF16)
        grad_query = own_features(inner(keys.T, d_scores)) * 0.125
        put(dq_ref, pair, grad_query.astype(BF16).T)
        key_terms = inner(d_scores, queries)
        value_terms = inner(probs_b, grads)
        for ref, at in ((dkl_ref, 0), (dk_ref, 1), (dkr_ref, 2)):
            put(ref, pair, key_terms[at * ROWS : (at + 1) * ROWS])
        for ref, at in ((dvl_ref, 0), (dv_ref, 1), (dvr_ref, 2)):
            put(ref, pair, value_terms[at * ROWS : (at + 1) * ROWS])


def sum_kernel(dk_ref, dv_ref, kl_ref, vl_ref, kr_ref, vr_ref, gk_ref, gv_ref):
    gk_ref[...] = (dk_ref[...] + kl_ref[...].astype(F32) + kr_ref[...].astype(F32)).astype(BF16)
    gv_ref[...] = (dv_ref[...] + vl_ref[...].astype(F32) + vr_ref[...].astype(F32)).astype(BF16)


def call(kernel, outs, args, flops, smem=0):
    moved = sum(a.size * a.dtype.itemsize for a in args)
    return pl.pallas_call(
        kernel,
        out_shape=outs,
        in_specs=[SMEM] * smem + [VMEM] * (len(args) - smem),
        out_specs=[VMEM] * len(outs),
        cost_estimate=pl.CostEstimate(flops=flops, bytes_accessed=moved, transcendentals=0),
        compiler_params=pltpu.CompilerParams(vmem_limit_bytes=40 * 2**20),
    )(*args)


def on_device(
    query_level, key_level, value_level, block_lists, query_column, key_column, grad_output
):
    size = lax.axis_size("lon")
    up = [(i, (i + 1) % size) for i in range(size)]
    down = [(j, i) for i, j in up]
    level = jax.ShapeDtypeStruct(query_level.shape, BF16)
    level32 = jax.ShapeDtypeStruct(query_level.shape, F32)
    column = jax.ShapeDtypeStruct(query_column.shape, BF16)
    key_left = lax.ppermute(key_level, "lon", up)
    key_right = lax.ppermute(key_level, "lon", down)
    value_left = lax.ppermute(value_level, "lon", up)
    value_right = lax.ppermute(value_level, "lon", down)
    unit = 2 * ROWS * ROWS * 1024
    (grad_col,) = call(
        column_forward, [column], [query_column, key_column, grad_output], 4 * unit
    )
    grad_att = lax.all_to_all(grad_col, "lev", split_axis=0, concat_axis=1, tiled=True)
    attended, grad_query, dk, dv, dkl, dvl, dkr, dvr = call(
        level_kernel,
        [level, level, level32, level32, level, level, level, level],
        [block_lists, query_level, key_level, value_level,
         key_left, value_left, key_right, value_right, grad_att],
        18 * unit,
        smem=1,
    )
    columns = lax.all_to_all(attended, "lev", split_axis=1, concat_axis=0, tiled=True)
    key_from_right = lax.ppermute(dkl, "lon", down)
    key_from_left = lax.ppermute(dkr, "lon", up)
    value_from_right = lax.ppermute(dvl, "lon", down)
    value_from_left = lax.ppermute(dvr, "lon", up)
    grad_query_column, grad_key_column = call(
        column_backward, [column, column], [query_column, key_column, grad_output, columns],
        6 * unit,
    )
    grad_key, grad_value = call(
        sum_kernel, [level, level],
        [dk, dv, key_from_left, value_from_left, key_from_right, value_from_right],
        unit,
    )
    return grad_query, grad_key, grad_value, grad_query_column, grad_key_column


def solution(mesh):
    level = P("lev", None, "lon", None)
    column = P(None, "lev", "lon", None)
    return jax.shard_map(
        on_device,
        mesh=mesh,
        in_specs=(level, level, level, P("lon", None, None), column, column, column),
        out_specs=(level, level, level, column, column),
        check_vma=False,
    )
```

```python
import jax
import jax.numpy as jnp
from jax import lax
from jax.experimental import pallas as pl
from jax.experimental.pallas import tpu as pltpu
from jax.sharding import PartitionSpec as P

PAIRS = 8
ROWS = 128
PAIR = 128
NEGATIVE = -1e30
F32 = jnp.float32
BF16 = jnp.bfloat16

VMEM = pl.BlockSpec(memory_space=pltpu.VMEM)
SMEM = pl.BlockSpec(memory_space=pltpu.SMEM)
ANY = pl.BlockSpec(memory_space=pl.ANY)


def tokens(ref, pair):
    return ref[:, :, :, pl.ds(pair * PAIR, PAIR)].reshape(ROWS, PAIR)


def put(ref, pair, value):
    shape = ref.shape[:-1] + (PAIR,)
    ref[:, :, :, pl.ds(pair * PAIR, PAIR)] = value.astype(ref.dtype).reshape(shape)


def both_heads(block):
    lane = lax.broadcasted_iota(jnp.int32, (1, PAIR), 1)
    first = (lane < PAIR // 2).astype(F32).astype(BF16)
    second = (lane >= PAIR // 2).astype(F32).astype(BF16)
    return jnp.concatenate([block * first, block * second], axis=0)


def outer(a, b):
    return lax.dot_general(a, b, (((1,), (1,)), ((), ())), preferred_element_type=F32)


def inner(a, b):
    return lax.dot_general(a, b, (((1,), (0,)), ((), ())), preferred_element_type=F32)


def own_features(both):
    half = PAIR // 2
    return jnp.concatenate([both[:half, :ROWS], both[half:, ROWS:]], axis=0)


def softmax_over_rows(scores):
    top = jnp.max(scores, axis=0, keepdims=True)
    raised = jnp.exp(scores - top)
    return raised * (1.0 / jnp.sum(raised, axis=0, keepdims=True))


def score_grads(probs, d_probs):
    return probs * (d_probs - jnp.sum(probs * d_probs, axis=0, keepdims=True))


def column_bias():
    key = lax.broadcasted_iota(jnp.int32, (ROWS, 2 * ROWS), 0)
    query = lax.broadcasted_iota(jnp.int32, (ROWS, 2 * ROWS), 1)
    return jnp.where((key & 15) == (query & 15), 0.0, NEGATIVE).astype(F32)


def column_forward(
    q_hbm, k_hbm, g_hbm, lk_hbm, lv_hbm, lq_hbm, out_ref, both_ref, lq_ref, q_ref, k_ref, g_ref, sems
):
    moves = [
        (q_hbm, q_ref),
        (k_hbm, k_ref),
        (g_hbm, g_ref),
        (lk_hbm, both_ref.at[pl.ds(0, 1)]),
        (lv_hbm, both_ref.at[pl.ds(1, 1)]),
        (lq_hbm, lq_ref),
    ]
    copies = [
        pltpu.make_async_copy(src, dst, sems.at[i]) for i, (src, dst) in enumerate(moves)
    ]
    for copy in copies:
        copy.start()
    bias = column_bias()
    for copy in copies[:3]:
        copy.wait()
    for pair in range(PAIRS):
        queries = both_heads(tokens(q_ref, pair) * BF16(0.125))
        probs = softmax_over_rows(outer(tokens(k_ref, pair), queries) + bias)
        put(out_ref, pair, inner(probs.astype(BF16), both_heads(tokens(g_ref, pair))))
    for copy in copies[3:]:
        copy.wait()


def send(pair, moves, sems):
    lanes = pl.ds(pair * PAIR, PAIR)
    copies = [
        pltpu.make_async_copy(src.at[:, :, :, lanes], dst.at[:, :, :, lanes], sems.at[i, pair])
        for i, (src, dst) in enumerate(moves)
    ]
    for copy in copies:
        copy.start()
    return copies


def final_kernel(
    q_ref, k_ref, g_ref, a_ref, dk_ref, dv_ref, near_ref, far_ref,
    dq_hbm, dkc_hbm, gk_hbm, gv_hbm, dqc_ref, dkc_ref, gk_ref, gv_ref, sems,
):
    bias = column_bias()
    copies = []
    for pair in range(PAIRS):
        lanes = pl.ds(pair * PAIR, PAIR)
        queries = both_heads(tokens(q_ref, pair) * BF16(0.125))
        keys = tokens(k_ref, pair)
        probs = softmax_over_rows(outer(keys, queries) + bias)
        d_probs = outer(tokens(a_ref, pair), both_heads(tokens(g_ref, pair)))
        d_scores = score_grads(probs, d_probs).astype(BF16)
        put(dkc_ref, pair, inner(d_scores, queries))
        grad_query = own_features(inner(keys.T, d_scores)) * 0.125
        put(dqc_ref, pair, grad_query.astype(BF16).T)
        for at, (own, out) in enumerate(((dk_ref, gk_ref), (dv_ref, gv_ref))):
            rims = near_ref[pl.ds(at, 1), :, :, lanes].astype(F32) + far_ref[pl.ds(at, 1), :, :, lanes].astype(F32)
            out[:, :, :, lanes] = (own[:, :, :, lanes] + rims).astype(BF16)
        moves = [(dqc_ref, dq_hbm), (dkc_ref, dkc_hbm), (gk_ref, gk_hbm), (gv_ref, gv_hbm)]
        copies += send(pair, moves, sems)
    for copy in copies:
        copy.wait()


def level_bias(lists_ref):
    odd = lax.axis_index("lon") % 2
    lane = lax.broadcasted_iota(jnp.int32, (1, ROWS), 1)
    listed = jnp.zeros((1, ROWS), jnp.int32)
    for block in range(4):
        bits = jnp.int32(0)
        for j in range(15):
            bits = bits | lax.shift_left(jnp.int32(1), lists_ref[0, block, j])
        listed = jnp.where(lane // 32 == block, bits, listed)
    row = lax.broadcasted_iota(jnp.int32, (ROWS, ROWS), 0)
    block = (row // 32) * 6 + (row % 4) // 2
    parts = []
    for part in (2 - 2 * odd, 1, 2 * odd):
        allowed = lax.shift_right_logical(jnp.broadcast_to(listed, row.shape), block + 2 * part)
        parts.append(jnp.where((allowed & 1) == 1, 0.0, NEGATIVE).astype(F32))
    bias = jnp.concatenate(parts, axis=0)
    return jnp.concatenate([bias, bias], axis=1)


def halo(near, own, far, at, pair):
    return jnp.concatenate([tokens(r.at[pl.ds(at, 1)], pair) for r in (near, own, far)], axis=0)


def level_kernel(
    lists_ref, q_ref, both_ref, near_ref, far_ref, g_ref,
    dq_hbm, att_ref, dk_ref, dv_ref, near_out, far_out, dq_ref, sems,
):
    bias = level_bias(lists_ref)
    copies = []
    for pair in range(PAIRS):
        queries = both_heads(tokens(q_ref, pair) * BF16(0.125))
        grads = both_heads(tokens(g_ref, pair))
        keys = halo(near_ref, both_ref, far_ref, 0, pair)
        values = halo(near_ref, both_ref, far_ref, 1, pair)
        probs = softmax_over_rows(outer(keys, queries) + bias)
        probs_b = probs.astype(BF16)
        attended = own_features(inner(values.T, probs_b))
        put(att_ref, pair, attended.astype(BF16).T)
        d_scores = score_grads(probs, outer(values, grads)).astype(BF16)
        grad_query = own_features(inner(keys.T, d_scores)) * 0.125
        put(dq_ref, pair, grad_query.astype(BF16).T)
        copies += send(pair, [(dq_ref, dq_hbm)], sems)
        key_terms = inner(d_scores, queries)
        value_terms = inner(probs_b, grads)
        put(near_out.at[pl.ds(0, 1)], pair, key_terms[:ROWS])
        put(near_out.at[pl.ds(1, 1)], pair, value_terms[:ROWS])
        put(dk_ref, pair, key_terms[ROWS : 2 * ROWS])
        put(dv_ref, pair, value_terms[ROWS : 2 * ROWS])
        put(far_out.at[pl.ds(0, 1)], pair, key_terms[2 * ROWS :])
        put(far_out.at[pl.ds(1, 1)], pair, value_terms[2 * ROWS :])
    for copy in copies:
        copy.wait()


def held(array):
    return pltpu.VMEM(array.shape, array.dtype)


def call(kernel, outs, args, units, smem=0, in_specs=None, out_specs=None, scratch=()):
    moved = sum(a.size * a.dtype.itemsize for a in args)
    if in_specs is None:
        args = args[:smem] + [pltpu.with_memory_space_constraint(a, pltpu.VMEM) for a in args[smem:]]
    return pl.pallas_call(
        kernel,
        out_shape=outs,
        in_specs=in_specs or [SMEM] * smem + [VMEM] * (len(args) - smem),
        out_specs=out_specs or [VMEM] * len(outs),
        scratch_shapes=scratch,
        cost_estimate=pl.CostEstimate(
            flops=units * 2 * ROWS * ROWS * 1024, bytes_accessed=moved, transcendentals=0
        ),
        compiler_params=pltpu.CompilerParams(vmem_limit_bytes=32 * 2**20),
    )(*args)


def on_device(
    query_level, key_level, value_level, block_lists, query_column, key_column, grad_output
):
    size = lax.axis_size("lon")
    near = [(i, i ^ 1) for i in range(size)]
    far = [(i, (i + 1) % size if i % 2 else (i - 1) % size) for i in range(size)]
    level = jax.ShapeDtypeStruct(query_level.shape, BF16)
    level32 = jax.ShapeDtypeStruct(query_level.shape, F32)
    column = jax.ShapeDtypeStruct(query_column.shape, BF16)
    two = jax.ShapeDtypeStruct((2,) + query_level.shape[1:], BF16)
    weights = jax.ShapeDtypeStruct((PAIRS, 3 * ROWS, 2 * ROWS), BF16)
    given = [query_column, key_column, grad_output, key_level, value_level, query_level]
    grad_col, both, queries, col_queries, col_keys, col_grads = call(
        column_forward,
        [held(column), held(two), held(level), held(column), held(column), held(column)],
        [pltpu.with_memory_space_constraint(a, pltpu.HBM) for a in given],
        4,
        in_specs=[ANY] * 6,
        scratch=[pltpu.SemaphoreType.DMA((6,))],
    )
    both_far = lax.ppermute(both, "lon", far)
    both_near = lax.ppermute(both, "lon", near)
    grad_att = lax.all_to_all(grad_col, "lev", split_axis=0, concat_axis=1, tiled=True)
    grad_query, attended, dk, dv, near_terms, far_terms = call(
        level_kernel,
        [level, held(level), held(level32), held(level32), held(two), held(two)],
        [block_lists, queries, both, both_near, both_far, grad_att],
        18,
        smem=1,
        out_specs=[ANY] + [VMEM] * 5,
        scratch=[pltpu.VMEM(level.shape, BF16), pltpu.SemaphoreType.DMA((1, PAIRS))],
    )
    far_sums = lax.ppermute(far_terms, "lon", far)
    near_sums = lax.ppermute(near_terms, "lon", near)
    columns = lax.all_to_all(attended, "lev", split_axis=1, concat_axis=0, tiled=True)
    grad_query_column, grad_key_column, grad_key, grad_value = call(
        final_kernel,
        [column, column, level, level],
        [col_queries, col_keys, col_grads, columns, dk, dv, near_sums, far_sums],
        8,
        out_specs=[ANY] * 4,
        scratch=[pltpu.VMEM(column.shape, BF16)] * 2 + [pltpu.VMEM(level.shape, BF16)] * 2
        + [pltpu.SemaphoreType.DMA((4, PAIRS))],
    )
    return grad_query, grad_key, grad_value, grad_query_column, grad_key_column


def solution(mesh):
    level = P("lev", None, "lon", None)
    column = P(None, "lev", "lon", None)
    return jax.shard_map(
        on_device,
        mesh=mesh,
        in_specs=(level, level, level, P("lon", None, None), column, column, column),
        out_specs=(level, level, level, column, column),
        check_vma=False,
    )
```

```python
import jax
import jax.numpy as jnp
from jax import lax
from jax.experimental import pallas as pl
from jax.experimental.pallas import tpu as pltpu
from jax.sharding import PartitionSpec as P

PAIRS = 8
ROWS = 128
PAIR = 128
NEGATIVE = -1e30
F32 = jnp.float32
BF16 = jnp.bfloat16

VMEM = pl.BlockSpec(memory_space=pltpu.VMEM)
ANY = pl.BlockSpec(memory_space=pl.ANY)


def tokens(ref, pair):
    return ref[:, :, :, pl.ds(pair * PAIR, PAIR)].reshape(ROWS, PAIR)


def put(ref, pair, value):
    shape = ref.shape[:-1] + (PAIR,)
    ref[:, :, :, pl.ds(pair * PAIR, PAIR)] = value.astype(ref.dtype).reshape(shape)


def both_heads(block):
    lane = lax.broadcasted_iota(jnp.int32, (1, PAIR), 1)
    first = (lane < PAIR // 2).astype(F32).astype(BF16)
    second = (lane >= PAIR // 2).astype(F32).astype(BF16)
    return jnp.concatenate([block * first, block * second], axis=0)


def outer(a, b):
    return lax.dot_general(a, b, (((1,), (1,)), ((), ())), preferred_element_type=F32)


def inner(a, b):
    return lax.dot_general(a, b, (((1,), (0,)), ((), ())), preferred_element_type=F32)


def own_features(both):
    half = PAIR // 2
    return jnp.concatenate([both[:half, :ROWS], both[half:, ROWS:]], axis=0)


def softmax_over_rows(scores):
    top = jnp.max(scores, axis=0, keepdims=True)
    raised = jnp.exp(scores - top)
    return raised * (1.0 / jnp.sum(raised, axis=0, keepdims=True))


def score_grads(probs, d_probs):
    return probs * (d_probs - jnp.sum(probs * d_probs, axis=0, keepdims=True))


def column_bias():
    key = lax.broadcasted_iota(jnp.int32, (ROWS, 2 * ROWS), 0)
    query = lax.broadcasted_iota(jnp.int32, (ROWS, 2 * ROWS), 1)
    return jnp.where((key & 15) == (query & 15), 0.0, NEGATIVE).astype(F32)


def pipelined(*stages):
    for step in range(PAIRS + len(stages) - 1):
        for delay in (0, 2, 1):
            if 0 <= step - delay < PAIRS:
                stages[delay](step - delay)


def level_bias(lists_ref):
    odd = lax.axis_index("lon") % 2
    lane = lax.broadcasted_iota(jnp.int32, (1, ROWS), 1)
    listed = jnp.zeros((1, ROWS), jnp.int32)
    for block in range(4):
        bits = jnp.int32(0)
        for j in range(15):
            bits = bits | lax.shift_left(jnp.int32(1), lists_ref[0, block, j])
        listed = jnp.where(lane // 32 == block, bits, listed)
    row = lax.broadcasted_iota(jnp.int32, (ROWS, ROWS), 0)
    block = (row // 32) * 6 + (row % 4) // 2
    parts = []
    for part in (2 - 2 * odd, 1, 2 * odd):
        allowed = lax.shift_right_logical(jnp.broadcast_to(listed, row.shape), block + 2 * part)
        parts.append(jnp.where((allowed & 1) == 1, 0.0, NEGATIVE).astype(F32))
    return jnp.concatenate(parts, axis=0)


def column_forward(
    lists_hbm, q_hbm, k_hbm, g_hbm, lk_hbm, lv_hbm, lq_hbm,
    out_ref, both_ref, lq_ref, q_ref, k_ref, g_ref, probs_ref, bias_ref,
    lists_ref, scores_ref, sems,
):
    moves = [
        (q_hbm, q_ref),
        (k_hbm, k_ref),
        (g_hbm, g_ref),
        (lists_hbm, lists_ref),
        (lk_hbm, both_ref.at[pl.ds(0, 1)]),
        (lv_hbm, both_ref.at[pl.ds(1, 1)]),
        (lq_hbm, lq_ref),
    ]
    copies = [
        pltpu.make_async_copy(src, dst, sems.at[i]) for i, (src, dst) in enumerate(moves)
    ]
    for copy in copies:
        copy.start()
    bias = column_bias()
    for copy in copies[:4]:
        copy.wait()

    def scores(pair):
        queries = both_heads(tokens(q_ref, pair) * BF16(0.125))
        scores_ref[pair % 2] = outer(tokens(k_ref, pair), queries)

    def softmax(pair):
        probs_ref[pair] = softmax_over_rows(scores_ref[pair % 2] + bias)

    def grads(pair):
        probs = probs_ref[pair].astype(BF16)
        put(out_ref, pair, inner(probs, both_heads(tokens(g_ref, pair))))

    pipelined(scores, softmax, grads)
    bias_ref[...] = level_bias(lists_ref)
    for copy in copies[4:]:
        copy.wait()


def send(pair, moves, sems):
    lanes = pl.ds(pair * PAIR, PAIR)
    copies = [
        pltpu.make_async_copy(src.at[:, :, :, lanes], dst.at[:, :, :, lanes], sems.at[i, pair])
        for i, (src, dst) in enumerate(moves)
    ]
    for copy in copies:
        copy.start()
    return copies


def final_kernel(
    q_ref, k_ref, g_ref, probs_ref, a_ref, dk_ref, dv_ref, near_ref, far_ref,
    dq_hbm, dkc_hbm, gk_hbm, gv_hbm, dqc_ref, dkc_ref, gk_ref, gv_ref, dp_ref, ds_ref, sems,
):
    copies = []

    def products(pair):
        dp_ref[pair % 2] = outer(tokens(a_ref, pair), both_heads(tokens(g_ref, pair)))

    def scores(pair):
        ds_ref[pair % 2] = score_grads(probs_ref[pair], dp_ref[pair % 2]).astype(BF16)

    def grads(pair):
        lanes = pl.ds(pair * PAIR, PAIR)
        d_scores = ds_ref[pair % 2]
        queries = both_heads(tokens(q_ref, pair) * BF16(0.125))
        put(dkc_ref, pair, inner(d_scores, queries))
        grad_query = own_features(inner(tokens(k_ref, pair).T, d_scores)) * 0.125
        put(dqc_ref, pair, grad_query.astype(BF16).T)
        for at, (own, out) in enumerate(((dk_ref, gk_ref), (dv_ref, gv_ref))):
            near = near_ref[pl.ds(at, 1), :, :, lanes].astype(F32)
            far = far_ref[pl.ds(at, 1), :, :, lanes].astype(F32)
            out[:, :, :, lanes] = (own[:, :, :, lanes] + (near + far)).astype(BF16)
        moves = [(dqc_ref, dq_hbm), (dkc_ref, dkc_hbm), (gk_ref, gk_hbm), (gv_ref, gv_hbm)]
        copies.extend(send(pair, moves, sems))

    pipelined(products, scores, grads)
    for copy in copies:
        copy.wait()


def halo(near, own, far, at, pair):
    return jnp.concatenate([tokens(r.at[pl.ds(at, 1)], pair) for r in (near, own, far)], axis=0)


def level_kernel(
    q_ref, both_ref, near_ref, far_ref, g_ref, bias_ref,
    dq_hbm, att_ref, dk_ref, dv_ref, near_out, far_out,
    dq_ref, s_ref, dp_ref, p_ref, ds_ref, qg_ref, kv_ref, sems,
):
    bias = jnp.concatenate([bias_ref[...], bias_ref[...]], axis=1)

    def products(pair):
        queries = both_heads(tokens(q_ref, pair) * BF16(0.125))
        grads = both_heads(tokens(g_ref, pair))
        keys = halo(near_ref, both_ref, far_ref, 0, pair)
        values = halo(near_ref, both_ref, far_ref, 1, pair)
        s_ref[pair % 2] = outer(keys, queries) + bias
        dp_ref[pair % 2] = outer(values, grads)
        qg_ref[pair % 4, 0] = queries
        qg_ref[pair % 4, 1] = grads
        kv_ref[pair % 4, 0] = keys.T
        kv_ref[pair % 4, 1] = values.T

    def scores(pair):
        probs = softmax_over_rows(s_ref[pair % 2])
        p_ref[pair % 2] = probs.astype(BF16)
        ds_ref[pair % 2] = score_grads(probs, dp_ref[pair % 2]).astype(BF16)

    def grads(pair):
        probs_b = p_ref[pair % 2]
        d_scores = ds_ref[pair % 2]
        attended = own_features(inner(kv_ref[pair % 4, 1], probs_b))
        grad_query = own_features(inner(kv_ref[pair % 4, 0], d_scores)) * 0.125
        key_terms = inner(d_scores, qg_ref[pair % 4, 0])
        value_terms = inner(probs_b, qg_ref[pair % 4, 1])
        put(att_ref, pair, attended.astype(BF16).T)
        put(dq_ref, pair, grad_query.astype(BF16).T)
        put(near_out.at[pl.ds(0, 1)], pair, key_terms[:ROWS])
        put(near_out.at[pl.ds(1, 1)], pair, value_terms[:ROWS])
        put(dk_ref, pair, key_terms[ROWS : 2 * ROWS])
        put(dv_ref, pair, value_terms[ROWS : 2 * ROWS])
        put(far_out.at[pl.ds(0, 1)], pair, key_terms[2 * ROWS :])
        put(far_out.at[pl.ds(1, 1)], pair, value_terms[2 * ROWS :])

    pipelined(products, scores, grads)
    copy = pltpu.make_async_copy(dq_ref, dq_hbm, sems.at[0])
    copy.start()
    copy.wait()


def held(array):
    return pltpu.VMEM(array.shape, array.dtype)


def call(kernel, outs, args, units, in_specs=None, out_specs=None, scratch=()):
    moved = sum(a.size * a.dtype.itemsize for a in args)
    if in_specs is None:
        args = [pltpu.with_memory_space_constraint(a, pltpu.VMEM) for a in args]
    return pl.pallas_call(
        kernel,
        out_shape=outs,
        in_specs=in_specs or [VMEM] * len(args),
        out_specs=out_specs or [VMEM] * len(outs),
        scratch_shapes=scratch,
        cost_estimate=pl.CostEstimate(
            flops=units * 2 * ROWS * ROWS * 1024, bytes_accessed=moved, transcendentals=0
        ),
        compiler_params=pltpu.CompilerParams(vmem_limit_bytes=32 * 2**20),
    )(*args)


def on_device(
    query_level, key_level, value_level, block_lists, query_column, key_column, grad_output
):
    size = lax.axis_size("lon")
    near = [(i, i ^ 1) for i in range(size)]
    far = [(i, (i + 1) % size if i % 2 else (i - 1) % size) for i in range(size)]
    level = jax.ShapeDtypeStruct(query_level.shape, BF16)
    level32 = jax.ShapeDtypeStruct(query_level.shape, F32)
    column = jax.ShapeDtypeStruct(query_column.shape, BF16)
    two = jax.ShapeDtypeStruct((2,) + query_level.shape[1:], BF16)
    col_probs = jax.ShapeDtypeStruct((PAIRS, ROWS, 2 * ROWS), F32)
    mask = jax.ShapeDtypeStruct((3 * ROWS, ROWS), F32)
    given = [
        block_lists, query_column, key_column, grad_output, key_level, value_level, query_level,
    ]
    grad_col, both, queries, col_queries, col_keys, col_grads, probs, bias = call(
        column_forward,
        [held(a) for a in (column, two, level, column, column, column, col_probs, mask)],
        [pltpu.with_memory_space_constraint(a, pltpu.HBM) for a in given],
        4,
        in_specs=[ANY] * 7,
        scratch=[
            pltpu.SMEM(block_lists.shape, jnp.int32),
            pltpu.VMEM((2, ROWS, 2 * ROWS), F32),
            pltpu.SemaphoreType.DMA((7,)),
        ],
    )
    both_far = lax.ppermute(both, "lon", far)
    both_near = lax.ppermute(both, "lon", near)
    grad_att = lax.all_to_all(grad_col, "lev", split_axis=0, concat_axis=1, tiled=True)
    grad_query, attended, dk, dv, near_terms, far_terms = call(
        level_kernel,
        [level] + [held(a) for a in (level, level32, level32, two, two)],
        [queries, both, both_near, both_far, grad_att, bias],
        18,
        out_specs=[ANY] + [VMEM] * 5,
        scratch=[
            pltpu.VMEM(level.shape, BF16),
            pltpu.VMEM((2, 3 * ROWS, 2 * ROWS), F32),
            pltpu.VMEM((2, 3 * ROWS, 2 * ROWS), F32),
            pltpu.VMEM((2, 3 * ROWS, 2 * ROWS), BF16),
            pltpu.VMEM((2, 3 * ROWS, 2 * ROWS), BF16),
            pltpu.VMEM((4, 2, 2 * ROWS, PAIR), BF16),
            pltpu.VMEM((4, 2, PAIR, 3 * ROWS), BF16),
            pltpu.SemaphoreType.DMA((1,)),
        ],
    )
    far_sums = lax.ppermute(far_terms, "lon", far)
    near_sums = lax.ppermute(near_terms, "lon", near)
    columns = lax.all_to_all(attended, "lev", split_axis=1, concat_axis=0, tiled=True)
    grad_query_column, grad_key_column, grad_key, grad_value = call(
        final_kernel,
        [column, column, level, level],
        [col_queries, col_keys, col_grads, probs, columns, dk, dv, near_sums, far_sums],
        8,
        out_specs=[ANY] * 4,
        scratch=[pltpu.VMEM(column.shape, BF16)] * 2
        + [pltpu.VMEM(level.shape, BF16)] * 2
        + [pltpu.VMEM((2, ROWS, 2 * ROWS), F32), pltpu.VMEM((2, ROWS, 2 * ROWS), BF16)]
        + [pltpu.SemaphoreType.DMA((4, PAIRS))],
    )
    return grad_query, grad_key, grad_value, grad_query_column, grad_key_column


def solution(mesh):
    level = P("lev", None, "lon", None)
    column = P(None, "lev", "lon", None)
    return jax.shard_map(
        on_device,
        mesh=mesh,
        in_specs=(level, level, level, P("lon", None, None), column, column, column),
        out_specs=(level, level, level, column, column),
        check_vma=False,
    )
```

```python
import jax
import jax.numpy as jnp
from jax import lax
from jax.experimental import pallas as pl
from jax.experimental.pallas import tpu as pltpu
from jax.sharding import PartitionSpec as P

PAIRS = 8
ROWS = 128
PAIR = 128
NEGATIVE = -1e30
F32 = jnp.float32
BF16 = jnp.bfloat16

VMEM = pl.BlockSpec(memory_space=pltpu.VMEM)
ANY = pl.BlockSpec(memory_space=pl.ANY)


def tokens(ref, pair):
    return ref[:, :, :, pl.ds(pair * PAIR, PAIR)].reshape(ROWS, PAIR)


def put(ref, pair, value):
    shape = ref.shape[:-1] + (PAIR,)
    ref[:, :, :, pl.ds(pair * PAIR, PAIR)] = value.astype(ref.dtype).reshape(shape)


def both_heads(block):
    lane = lax.broadcasted_iota(jnp.int32, (1, PAIR), 1)
    first = (lane < PAIR // 2).astype(F32).astype(BF16)
    second = (lane >= PAIR // 2).astype(F32).astype(BF16)
    return jnp.concatenate([block * first, block * second], axis=0)


def outer(a, b):
    return lax.dot_general(a, b, (((1,), (1,)), ((), ())), preferred_element_type=F32)


def inner(a, b):
    return lax.dot_general(a, b, (((1,), (0,)), ((), ())), preferred_element_type=F32)


def own_features(both):
    half = PAIR // 2
    return jnp.concatenate([both[:half, :ROWS], both[half:, ROWS:]], axis=0)


def softmax_over_rows(scores):
    top = jnp.max(scores, axis=0, keepdims=True)
    raised = jnp.exp(scores - top)
    return raised * (1.0 / jnp.sum(raised, axis=0, keepdims=True))


def score_grads(probs, d_probs):
    return probs * (d_probs - jnp.sum(probs * d_probs, axis=0, keepdims=True))


def column_bias():
    key = lax.broadcasted_iota(jnp.int32, (ROWS, 2 * ROWS), 0)
    query = lax.broadcasted_iota(jnp.int32, (ROWS, 2 * ROWS), 1)
    return jnp.where((key & 15) == (query & 15), 0.0, NEGATIVE).astype(F32)


def pipelined(*stages):
    for step in range(PAIRS + len(stages) - 1):
        for delay in (0, 2, 1):
            if 0 <= step - delay < PAIRS:
                stages[delay](step - delay)


def level_bias(lists_ref):
    odd = lax.axis_index("lon") % 2
    lane = lax.broadcasted_iota(jnp.int32, (1, ROWS), 1)
    listed = jnp.zeros((1, ROWS), jnp.int32)
    for block in range(4):
        bits = jnp.int32(0)
        for j in range(15):
            bits = bits | lax.shift_left(jnp.int32(1), lists_ref[0, block, j])
        listed = jnp.where(lane // 32 == block, bits, listed)
    row = lax.broadcasted_iota(jnp.int32, (ROWS, ROWS), 0)
    block = (row // 32) * 6 + (row % 4) // 2
    parts = []
    for part in (2 - 2 * odd, 1, 2 * odd):
        allowed = lax.shift_right_logical(jnp.broadcast_to(listed, row.shape), block + 2 * part)
        parts.append(jnp.where((allowed & 1) == 1, 0.0, NEGATIVE).astype(F32))
    return jnp.concatenate(parts, axis=0)


def column_forward(
    lists_hbm, q_hbm, k_hbm, g_hbm, lk_hbm, lv_hbm, lq_hbm,
    out_ref, both_ref, lq_ref, q_ref, k_ref, g_ref, probs_ref, bias_ref,
    lists_ref, scores_ref, sems,
):
    moves = [
        (lists_hbm, lists_ref),
        (q_hbm, q_ref),
        (k_hbm, k_ref),
        (g_hbm, g_ref),
        (lk_hbm, both_ref.at[pl.ds(0, 1)]),
        (lv_hbm, both_ref.at[pl.ds(1, 1)]),
        (lq_hbm, lq_ref),
    ]
    copies = [
        pltpu.make_async_copy(src, dst, sems.at[i]) for i, (src, dst) in enumerate(moves)
    ]
    for copy in copies:
        copy.start()
    copies[0].wait()
    bias_ref[...] = level_bias(lists_ref)
    bias = column_bias()
    for copy in copies[1:4]:
        copy.wait()

    def scores(pair):
        queries = both_heads(tokens(q_ref, pair) * BF16(0.125))
        scores_ref[pair % 2] = outer(tokens(k_ref, pair), queries)

    def softmax(pair):
        probs_ref[pair] = softmax_over_rows(scores_ref[pair % 2] + bias)

    def grads(pair):
        probs = probs_ref[pair].astype(BF16)
        put(out_ref, pair, inner(probs, both_heads(tokens(g_ref, pair))))

    pipelined(scores, softmax, grads)
    for copy in copies[4:]:
        copy.wait()


def send(pair, moves, sems):
    lanes = pl.ds(pair * PAIR, PAIR)
    copies = [
        pltpu.make_async_copy(src.at[:, :, :, lanes], dst.at[:, :, :, lanes], sems.at[i, pair])
        for i, (src, dst) in enumerate(moves)
    ]
    for copy in copies:
        copy.start()
    return copies


def final_kernel(
    q_ref, k_ref, g_ref, probs_ref, a_ref, dk_ref, dv_ref, near_ref, far_ref, lq_ref,
    dq_hbm, dkc_hbm, gk_hbm, gv_hbm, lq_hbm,
    dqc_ref, dkc_ref, gk_ref, gv_ref, dp_ref, ds_ref, sems, lq_sem,
):
    copies = [pltpu.make_async_copy(lq_ref, lq_hbm, lq_sem.at[0])]
    copies[0].start()

    def products(pair):
        dp_ref[pair % 2] = outer(tokens(a_ref, pair), both_heads(tokens(g_ref, pair)))

    def scores(pair):
        ds_ref[pair % 2] = score_grads(probs_ref[pair], dp_ref[pair % 2]).astype(BF16)

    def grads(pair):
        lanes = pl.ds(pair * PAIR, PAIR)
        d_scores = ds_ref[pair % 2]
        queries = both_heads(tokens(q_ref, pair) * BF16(0.125))
        put(dkc_ref, pair, inner(d_scores, queries))
        grad_query = own_features(inner(tokens(k_ref, pair).T, d_scores)) * 0.125
        put(dqc_ref, pair, grad_query.astype(BF16).T)
        for at, (own, out) in enumerate(((dk_ref, gk_ref), (dv_ref, gv_ref))):
            near = near_ref[pl.ds(at, 1), :, :, lanes].astype(F32)
            far = far_ref[pl.ds(at, 1), :, :, lanes].astype(F32)
            out[:, :, :, lanes] = (own[:, :, :, lanes] + (near + far)).astype(BF16)
        moves = [(dqc_ref, dq_hbm), (dkc_ref, dkc_hbm), (gk_ref, gk_hbm), (gv_ref, gv_hbm)]
        copies.extend(send(pair, moves, sems))

    pipelined(products, scores, grads)
    for copy in copies:
        copy.wait()


def halo(near, own, far, at, pair):
    return jnp.concatenate([tokens(r.at[pl.ds(at, 1)], pair) for r in (near, own, far)], axis=0)


def level_kernel(
    q_ref, both_ref, near_ref, far_ref, g_ref, bias_ref,
    dq_ref, att_ref, dk_ref, dv_ref, near_out, far_out,
    s_ref, dp_ref, p_ref, ds_ref, qg_ref, kv_ref,
):
    bias = jnp.concatenate([bias_ref[...], bias_ref[...]], axis=1)

    def products(pair):
        queries = both_heads(tokens(q_ref, pair) * BF16(0.125))
        grads = both_heads(tokens(g_ref, pair))
        keys = halo(near_ref, both_ref, far_ref, 0, pair)
        values = halo(near_ref, both_ref, far_ref, 1, pair)
        s_ref[pair % 2] = outer(keys, queries) + bias
        dp_ref[pair % 2] = outer(values, grads)
        qg_ref[pair % 4, 0] = queries
        qg_ref[pair % 4, 1] = grads
        kv_ref[pair % 4, 0] = keys.T
        kv_ref[pair % 4, 1] = values.T

    def scores(pair):
        probs = softmax_over_rows(s_ref[pair % 2])
        p_ref[pair % 2] = probs.astype(BF16)
        ds_ref[pair % 2] = score_grads(probs, dp_ref[pair % 2]).astype(BF16)

    def grads(pair):
        probs_b = p_ref[pair % 2]
        d_scores = ds_ref[pair % 2]
        attended = own_features(inner(kv_ref[pair % 4, 1], probs_b))
        grad_query = own_features(inner(kv_ref[pair % 4, 0], d_scores)) * 0.125
        key_terms = inner(d_scores, qg_ref[pair % 4, 0])
        value_terms = inner(probs_b, qg_ref[pair % 4, 1])
        put(att_ref, pair, attended.astype(BF16).T)
        put(dq_ref, pair, grad_query.astype(BF16).T)
        put(near_out.at[pl.ds(0, 1)], pair, key_terms[:ROWS])
        put(near_out.at[pl.ds(1, 1)], pair, value_terms[:ROWS])
        put(dk_ref, pair, key_terms[ROWS : 2 * ROWS])
        put(dv_ref, pair, value_terms[ROWS : 2 * ROWS])
        put(far_out.at[pl.ds(0, 1)], pair, key_terms[2 * ROWS :])
        put(far_out.at[pl.ds(1, 1)], pair, value_terms[2 * ROWS :])

    pipelined(products, scores, grads)


def held(array):
    return pltpu.VMEM(array.shape, array.dtype)


def call(kernel, outs, args, units, in_specs=None, out_specs=None, scratch=()):
    moved = sum(a.size * a.dtype.itemsize for a in args)
    if in_specs is None:
        args = [pltpu.with_memory_space_constraint(a, pltpu.VMEM) for a in args]
    return pl.pallas_call(
        kernel,
        out_shape=outs,
        in_specs=in_specs or [VMEM] * len(args),
        out_specs=out_specs or [VMEM] * len(outs),
        scratch_shapes=scratch,
        cost_estimate=pl.CostEstimate(
            flops=units * 2 * ROWS * ROWS * 1024, bytes_accessed=moved, transcendentals=0
        ),
        compiler_params=pltpu.CompilerParams(vmem_limit_bytes=32 * 2**20),
    )(*args)


def on_device(
    query_level, key_level, value_level, block_lists, query_column, key_column, grad_output
):
    size = lax.axis_size("lon")
    near = [(i, i ^ 1) for i in range(size)]
    far = [(i, (i + 1) % size if i % 2 else (i - 1) % size) for i in range(size)]
    level = jax.ShapeDtypeStruct(query_level.shape, BF16)
    level32 = jax.ShapeDtypeStruct(query_level.shape, F32)
    column = jax.ShapeDtypeStruct(query_column.shape, BF16)
    two = jax.ShapeDtypeStruct((2,) + query_level.shape[1:], BF16)
    col_probs = jax.ShapeDtypeStruct((PAIRS, ROWS, 2 * ROWS), F32)
    mask = jax.ShapeDtypeStruct((3 * ROWS, ROWS), F32)
    given = [
        block_lists, query_column, key_column, grad_output, key_level, value_level, query_level,
    ]
    grad_col, both, queries, col_queries, col_keys, col_grads, probs, bias = call(
        column_forward,
        [held(a) for a in (column, two, level, column, column, column, col_probs, mask)],
        [pltpu.with_memory_space_constraint(a, pltpu.HBM) for a in given],
        4,
        in_specs=[ANY] * 7,
        scratch=[
            pltpu.SMEM(block_lists.shape, jnp.int32),
            pltpu.VMEM((2, ROWS, 2 * ROWS), F32),
            pltpu.SemaphoreType.DMA((7,)),
        ],
    )
    both_near = lax.ppermute(both, "lon", near)
    both_far = lax.ppermute(both, "lon", far)
    grad_att = lax.all_to_all(grad_col, "lev", split_axis=0, concat_axis=1, tiled=True)
    grad_query, attended, dk, dv, near_terms, far_terms = call(
        level_kernel,
        [held(a) for a in (level, level, level32, level32, two, two)],
        [queries, both, both_near, both_far, grad_att, bias],
        18,
        scratch=[
            pltpu.VMEM((2, 3 * ROWS, 2 * ROWS), F32),
            pltpu.VMEM((2, 3 * ROWS, 2 * ROWS), F32),
            pltpu.VMEM((2, 3 * ROWS, 2 * ROWS), BF16),
            pltpu.VMEM((2, 3 * ROWS, 2 * ROWS), BF16),
            pltpu.VMEM((4, 2, 2 * ROWS, PAIR), BF16),
            pltpu.VMEM((4, 2, PAIR, 3 * ROWS), BF16),
        ],
    )
    far_sums = lax.ppermute(far_terms, "lon", far)
    near_sums = lax.ppermute(near_terms, "lon", near)
    columns = lax.all_to_all(attended, "lev", split_axis=1, concat_axis=0, tiled=True)
    grad_query_column, grad_key_column, grad_key, grad_value, grad_query = call(
        final_kernel,
        [column, column, level, level, level],
        [
            col_queries, col_keys, col_grads, probs, columns,
            dk, dv, near_sums, far_sums, grad_query,
        ],
        8,
        out_specs=[ANY] * 5,
        scratch=[pltpu.VMEM(column.shape, BF16)] * 2
        + [pltpu.VMEM(level.shape, BF16)] * 2
        + [pltpu.VMEM((2, ROWS, 2 * ROWS), F32), pltpu.VMEM((2, ROWS, 2 * ROWS), BF16)]
        + [pltpu.SemaphoreType.DMA((4, PAIRS)), pltpu.SemaphoreType.DMA((1,))],
    )
    return grad_query, grad_key, grad_value, grad_query_column, grad_key_column


def solution(mesh):
    level = P("lev", None, "lon", None)
    column = P(None, "lev", "lon", None)
    return jax.shard_map(
        on_device,
        mesh=mesh,
        in_specs=(level, level, level, P("lon", None, None), column, column, column),
        out_specs=(level, level, level, column, column),
        check_vma=False,
    )
```

```python
import jax
import jax.numpy as jnp
from jax import lax
from jax.experimental import pallas as pl
from jax.experimental.pallas import tpu as pltpu
from jax.sharding import PartitionSpec as P

PAIRS = 8
ROWS = 128
PAIR = 128
NEGATIVE = -1e30
F32 = jnp.float32
BF16 = jnp.bfloat16

VMEM = pl.BlockSpec(memory_space=pltpu.VMEM)
ANY = pl.BlockSpec(memory_space=pl.ANY)


def tokens(ref, pair):
    return ref[:, :, :, pl.ds(pair * PAIR, PAIR)].reshape(ROWS, PAIR)


def put(ref, pair, value):
    shape = ref.shape[:-1] + (PAIR,)
    ref[:, :, :, pl.ds(pair * PAIR, PAIR)] = value.astype(ref.dtype).reshape(shape)


def both_heads(block):
    lane = lax.broadcasted_iota(jnp.int32, (1, PAIR), 1)
    first = (lane < PAIR // 2).astype(F32).astype(BF16)
    second = (lane >= PAIR // 2).astype(F32).astype(BF16)
    return jnp.concatenate([block * first, block * second], axis=0)


def outer(a, b):
    return lax.dot_general(a, b, (((1,), (1,)), ((), ())), preferred_element_type=F32)


def inner(a, b):
    return lax.dot_general(a, b, (((1,), (0,)), ((), ())), preferred_element_type=F32)


def own_features(both):
    half = PAIR // 2
    return jnp.concatenate([both[:half, :ROWS], both[half:, ROWS:]], axis=0)


def softmax_over_rows(scores):
    top = jnp.max(scores, axis=0, keepdims=True)
    raised = jnp.exp(scores - top)
    return raised * (1.0 / jnp.sum(raised, axis=0, keepdims=True))


def score_grads(probs, d_probs):
    return probs * (d_probs - jnp.sum(probs * d_probs, axis=0, keepdims=True))


def column_bias():
    key = lax.broadcasted_iota(jnp.int32, (ROWS, 2 * ROWS), 0)
    query = lax.broadcasted_iota(jnp.int32, (ROWS, 2 * ROWS), 1)
    return jnp.where((key & 15) == (query & 15), 0.0, NEGATIVE).astype(F32)


def pipelined(*stages):
    for step in range(PAIRS + len(stages) - 1):
        for delay in (0, 2, 1):
            if 0 <= step - delay < PAIRS:
                stages[delay](step - delay)


def level_bias(lists_ref):
    odd = lax.axis_index("lon") % 2
    lane = lax.broadcasted_iota(jnp.int32, (1, ROWS), 1)
    listed = jnp.zeros((1, ROWS), jnp.int32)
    for block in range(4):
        bits = jnp.int32(0)
        for j in range(15):
            bits = bits | lax.shift_left(jnp.int32(1), lists_ref[0, block, j])
        listed = jnp.where(lane // 32 == block, bits, listed)
    row = lax.broadcasted_iota(jnp.int32, (ROWS, ROWS), 0)
    block = (row // 32) * 6 + (row % 4) // 2
    parts = []
    for part in (2 - 2 * odd, 1, 2 * odd):
        allowed = lax.shift_right_logical(jnp.broadcast_to(listed, row.shape), block + 2 * part)
        parts.append(jnp.where((allowed & 1) == 1, 0.0, NEGATIVE).astype(F32))
    return jnp.concatenate(parts, axis=0)


def column_forward(
    lists_hbm, q_hbm, k_hbm, g_hbm, lk_hbm, lv_hbm, lq_hbm,
    out_ref, both_ref, lq_ref, q_ref, k_ref, g_ref, probs_ref, bias_ref,
    lists_ref, scores_ref, sems,
):
    moves = [
        (lists_hbm, lists_ref),
        (q_hbm, q_ref),
        (k_hbm, k_ref),
        (g_hbm, g_ref),
        (lk_hbm, both_ref.at[pl.ds(0, 1)]),
        (lv_hbm, both_ref.at[pl.ds(1, 1)]),
        (lq_hbm, lq_ref),
    ]
    copies = [
        pltpu.make_async_copy(src, dst, sems.at[i]) for i, (src, dst) in enumerate(moves)
    ]
    for copy in copies:
        copy.start()
    copies[0].wait()
    bias_ref[...] = level_bias(lists_ref)
    bias = column_bias()
    for copy in copies[1:4]:
        copy.wait()

    def scores(pair):
        queries = both_heads(tokens(q_ref, pair) * BF16(0.125))
        scores_ref[pair % 2] = outer(tokens(k_ref, pair), queries)

    def softmax(pair):
        probs_ref[pair] = softmax_over_rows(scores_ref[pair % 2] + bias)

    def grads(pair):
        probs = probs_ref[pair].astype(BF16)
        put(out_ref, pair, inner(probs, both_heads(tokens(g_ref, pair))))

    pipelined(scores, softmax, grads)
    for copy in copies[4:]:
        copy.wait()


def final_kernel(
    q_ref, k_ref, g_ref, probs_ref, a_ref, dk_ref, dv_ref, near_ref, far_ref, lq_ref,
    dq_hbm, dkc_hbm, gk_hbm, gv_hbm, lq_hbm,
    dqc_ref, dkc_ref, gk_ref, gv_ref, dp_ref, ds_ref, sems,
):
    copies = [pltpu.make_async_copy(lq_ref, lq_hbm, sems.at[0])]
    copies[0].start()

    def products(pair):
        dp_ref[pair % 2] = outer(tokens(a_ref, pair), both_heads(tokens(g_ref, pair)))

    def scores(pair):
        ds_ref[pair % 2] = score_grads(probs_ref[pair], dp_ref[pair % 2]).astype(BF16)

    def grads(pair):
        d_scores = ds_ref[pair % 2]
        queries = both_heads(tokens(q_ref, pair) * BF16(0.125))
        put(dkc_ref, pair, inner(d_scores, queries))
        grad_query = own_features(inner(tokens(k_ref, pair).T, d_scores)) * 0.125
        put(dqc_ref, pair, grad_query.astype(BF16).T)

    for at, (own, out, hbm) in enumerate(((dk_ref, gk_ref, gk_hbm), (dv_ref, gv_ref, gv_hbm))):
        rims = near_ref[pl.ds(at, 1)].astype(F32) + far_ref[pl.ds(at, 1)].astype(F32)
        out[...] = (own[...] + rims).astype(BF16)
        copies.append(pltpu.make_async_copy(out, hbm, sems.at[1 + at]))
        copies[-1].start()
    pipelined(products, scores, grads)
    for at, (out, hbm) in enumerate(((dqc_ref, dq_hbm), (dkc_ref, dkc_hbm))):
        copies.append(pltpu.make_async_copy(out, hbm, sems.at[3 + at]))
        copies[-1].start()
    for copy in copies:
        copy.wait()


def halo(near, own, far, at, pair):
    parts = (near, own.at[pl.ds(at, 1)], far.at[pl.ds(at, 1)])
    return jnp.concatenate([tokens(part, pair) for part in parts], axis=0)


def level_kernel(
    q_ref, both_ref, near_k, near_v, far_ref, g_ref, bias_ref,
    dq_ref, att_ref, dk_ref, dv_ref, near_out, far_out,
    s_ref, dp_ref, p_ref, ds_ref, qg_ref, kv_ref,
):
    bias = jnp.concatenate([bias_ref[...], bias_ref[...]], axis=1)

    def products(pair):
        queries = both_heads(tokens(q_ref, pair) * BF16(0.125))
        grads = both_heads(tokens(g_ref, pair))
        keys = halo(near_k, both_ref, far_ref, 0, pair)
        values = halo(near_v, both_ref, far_ref, 1, pair)
        s_ref[pair % 2] = outer(keys, queries) + bias
        dp_ref[pair % 2] = outer(values, grads)
        qg_ref[pair % 4, 0] = queries
        qg_ref[pair % 4, 1] = grads
        kv_ref[pair % 4, 0] = keys.T
        kv_ref[pair % 4, 1] = values.T

    def scores(pair):
        probs = softmax_over_rows(s_ref[pair % 2])
        p_ref[pair % 2] = probs.astype(BF16)
        ds_ref[pair % 2] = score_grads(probs, dp_ref[pair % 2]).astype(BF16)

    def grads(pair):
        probs_b = p_ref[pair % 2]
        d_scores = ds_ref[pair % 2]
        attended = own_features(inner(kv_ref[pair % 4, 1], probs_b))
        grad_query = own_features(inner(kv_ref[pair % 4, 0], d_scores)) * 0.125
        key_terms = inner(d_scores, qg_ref[pair % 4, 0])
        value_terms = inner(probs_b, qg_ref[pair % 4, 1])
        put(att_ref, pair, attended.astype(BF16).T)
        put(dq_ref, pair, grad_query.astype(BF16).T)
        put(near_out.at[pl.ds(0, 1)], pair, key_terms[:ROWS])
        put(near_out.at[pl.ds(1, 1)], pair, value_terms[:ROWS])
        put(dk_ref, pair, key_terms[ROWS : 2 * ROWS])
        put(dv_ref, pair, value_terms[ROWS : 2 * ROWS])
        put(far_out.at[pl.ds(0, 1)], pair, key_terms[2 * ROWS :])
        put(far_out.at[pl.ds(1, 1)], pair, value_terms[2 * ROWS :])

    pipelined(products, scores, grads)


def held(array):
    return pltpu.VMEM(array.shape, array.dtype)


def call(kernel, outs, args, units, in_specs=None, out_specs=None, scratch=()):
    moved = sum(a.size * a.dtype.itemsize for a in args)
    if in_specs is None:
        args = [pltpu.with_memory_space_constraint(a, pltpu.VMEM) for a in args]
    return pl.pallas_call(
        kernel,
        out_shape=outs,
        in_specs=in_specs or [VMEM] * len(args),
        out_specs=out_specs or [VMEM] * len(outs),
        scratch_shapes=scratch,
        cost_estimate=pl.CostEstimate(
            flops=units * 2 * ROWS * ROWS * 1024, bytes_accessed=moved, transcendentals=0
        ),
        compiler_params=pltpu.CompilerParams(vmem_limit_bytes=32 * 2**20),
    )(*args)


def on_device(
    query_level, key_level, value_level, block_lists, query_column, key_column, grad_output
):
    size = lax.axis_size("lon")
    near = [(i, i ^ 1) for i in range(size)]
    far = [(i, (i + 1) % size if i % 2 else (i - 1) % size) for i in range(size)]
    level = jax.ShapeDtypeStruct(query_level.shape, BF16)
    level32 = jax.ShapeDtypeStruct(query_level.shape, F32)
    column = jax.ShapeDtypeStruct(query_column.shape, BF16)
    two = jax.ShapeDtypeStruct((2,) + query_level.shape[1:], BF16)
    col_probs = jax.ShapeDtypeStruct((PAIRS, ROWS, 2 * ROWS), F32)
    mask = jax.ShapeDtypeStruct((3 * ROWS, ROWS), F32)
    given = [
        block_lists, query_column, key_column, grad_output, key_level, value_level, query_level,
    ]
    near_k = lax.ppermute(key_level, "lon", near)
    near_v = lax.ppermute(value_level, "lon", near)
    grad_col, both, queries, col_queries, col_keys, col_grads, probs, bias = call(
        column_forward,
        [held(a) for a in (column, two, level, column, column, column, col_probs, mask)],
        [pltpu.with_memory_space_constraint(a, pltpu.HBM) for a in given],
        4,
        in_specs=[ANY] * 7,
        scratch=[
            pltpu.SMEM(block_lists.shape, jnp.int32),
            pltpu.VMEM((2, ROWS, 2 * ROWS), F32),
            pltpu.SemaphoreType.DMA((7,)),
        ],
    )
    shared, near_k, near_v = lax.optimization_barrier((both, near_k, near_v))
    both_far = lax.ppermute(shared, "lon", far)
    grad_att = lax.all_to_all(grad_col, "lev", split_axis=0, concat_axis=1, tiled=True)
    grad_query, attended, dk, dv, near_terms, far_terms = call(
        level_kernel,
        [held(a) for a in (level, level, level32, level32, two, two)],
        [queries, both, near_k, near_v, both_far, grad_att, bias],
        18,
        scratch=[
            pltpu.VMEM((2, 3 * ROWS, 2 * ROWS), F32),
            pltpu.VMEM((2, 3 * ROWS, 2 * ROWS), F32),
            pltpu.VMEM((2, 3 * ROWS, 2 * ROWS), BF16),
            pltpu.VMEM((2, 3 * ROWS, 2 * ROWS), BF16),
            pltpu.VMEM((4, 2, 2 * ROWS, PAIR), BF16),
            pltpu.VMEM((4, 2, PAIR, 3 * ROWS), BF16),
        ],
    )
    far_sums = lax.ppermute(far_terms, "lon", far)
    near_sums = lax.ppermute(near_terms, "lon", near)
    columns = lax.all_to_all(attended, "lev", split_axis=1, concat_axis=0, tiled=True)
    grad_query_column, grad_key_column, grad_key, grad_value, grad_query = call(
        final_kernel,
        [column, column, level, level, level],
        [
            col_queries, col_keys, col_grads, probs, columns,
            dk, dv, near_sums, far_sums, grad_query,
        ],
        8,
        out_specs=[ANY] * 5,
        scratch=[pltpu.VMEM(column.shape, BF16)] * 2
        + [pltpu.VMEM(level.shape, BF16)] * 2
        + [pltpu.VMEM((2, ROWS, 2 * ROWS), F32), pltpu.VMEM((2, ROWS, 2 * ROWS), BF16)]
        + [pltpu.SemaphoreType.DMA((5,))],
    )
    return grad_query, grad_key, grad_value, grad_query_column, grad_key_column


def solution(mesh):
    level = P("lev", None, "lon", None)
    column = P(None, "lev", "lon", None)
    return jax.shard_map(
        on_device,
        mesh=mesh,
        in_specs=(level, level, level, P("lon", None, None), column, column, column),
        out_specs=(level, level, level, column, column),
        check_vma=False,
    )
```

```python
import jax
import jax.numpy as jnp
from jax import lax
from jax.experimental import pallas as pl
from jax.experimental.pallas import tpu as pltpu
from jax.sharding import PartitionSpec as P

PAIRS = 8
ROWS = 128
PAIR = 128
NEGATIVE = -1e30
F32 = jnp.float32
BF16 = jnp.bfloat16

VMEM = pl.BlockSpec(memory_space=pltpu.VMEM)
ANY = pl.BlockSpec(memory_space=pl.ANY)


def tokens(ref, pair):
    return ref[:, :, :, pl.ds(pair * PAIR, PAIR)].reshape(ROWS, PAIR)


def put(ref, pair, value):
    shape = ref.shape[:-1] + (PAIR,)
    ref[:, :, :, pl.ds(pair * PAIR, PAIR)] = value.astype(ref.dtype).reshape(shape)


def both_heads(block):
    lane = lax.broadcasted_iota(jnp.int32, (1, PAIR), 1)
    first = (lane < PAIR // 2).astype(F32).astype(BF16)
    second = (lane >= PAIR // 2).astype(F32).astype(BF16)
    return jnp.concatenate([block * first, block * second], axis=0)


def outer(a, b):
    return lax.dot_general(a, b, (((1,), (1,)), ((), ())), preferred_element_type=F32)


def inner(a, b):
    return lax.dot_general(a, b, (((1,), (0,)), ((), ())), preferred_element_type=F32)


def own_features(both):
    half = PAIR // 2
    return jnp.concatenate([both[:half, :ROWS], both[half:, ROWS:]], axis=0)


def softmax_over_rows(scores):
    top = jnp.max(scores, axis=0, keepdims=True)
    raised = jnp.exp(scores - top)
    return raised * (1.0 / jnp.sum(raised, axis=0, keepdims=True))


def score_grads(probs, d_probs):
    return probs * (d_probs - jnp.sum(probs * d_probs, axis=0, keepdims=True))


def column_bias():
    key = lax.broadcasted_iota(jnp.int32, (ROWS, 2 * ROWS), 0)
    query = lax.broadcasted_iota(jnp.int32, (ROWS, 2 * ROWS), 1)
    return jnp.where((key & 15) == (query & 15), 0.0, NEGATIVE).astype(F32)


def pipelined(*stages):
    for step in range(PAIRS + len(stages) - 1):
        for delay in (0, 2, 1):
            if 0 <= step - delay < PAIRS:
                stages[delay](step - delay)


def level_bias(lists_ref):
    odd = lax.axis_index("lon") % 2
    lane = lax.broadcasted_iota(jnp.int32, (1, ROWS), 1)
    listed = jnp.zeros((1, ROWS), jnp.int32)
    for block in range(4):
        bits = jnp.int32(0)
        for j in range(15):
            bits = bits | lax.shift_left(jnp.int32(1), lists_ref[0, block, j])
        listed = jnp.where(lane // 32 == block, bits, listed)
    row = lax.broadcasted_iota(jnp.int32, (ROWS, ROWS), 0)
    block = (row // 32) * 6 + (row % 4) // 2
    parts = []
    for part in (2 - 2 * odd, 1, 2 * odd):
        allowed = lax.shift_right_logical(jnp.broadcast_to(listed, row.shape), block + 2 * part)
        parts.append(jnp.where((allowed & 1) == 1, 0.0, NEGATIVE).astype(F32))
    return jnp.concatenate(parts, axis=0)


def column_forward(
    lists_hbm, q_hbm, k_hbm, g_hbm, lk_hbm, lv_hbm, lq_hbm,
    out_ref, both_ref, lq_ref, q_ref, k_ref, g_ref, probs_ref, bias_ref,
    lists_ref, scores_ref, sems,
):
    moves = [
        (lists_hbm, lists_ref),
        (q_hbm, q_ref),
        (k_hbm, k_ref),
        (g_hbm, g_ref),
        (lk_hbm, both_ref.at[pl.ds(0, 1)]),
        (lv_hbm, both_ref.at[pl.ds(1, 1)]),
        (lq_hbm, lq_ref),
    ]
    copies = [
        pltpu.make_async_copy(src, dst, sems.at[i]) for i, (src, dst) in enumerate(moves)
    ]
    for copy in copies:
        copy.start()
    copies[0].wait()
    bias_ref[...] = level_bias(lists_ref)
    bias = column_bias()
    for copy in copies[1:4]:
        copy.wait()

    def scores(pair):
        queries = both_heads(tokens(q_ref, pair) * BF16(0.125))
        scores_ref[pair % 2] = outer(tokens(k_ref, pair), queries)

    def softmax(pair):
        probs_ref[pair] = softmax_over_rows(scores_ref[pair % 2] + bias)

    def grads(pair):
        probs = probs_ref[pair].astype(BF16)
        put(out_ref, pair, inner(probs, both_heads(tokens(g_ref, pair))))

    pipelined(scores, softmax, grads)
    for copy in copies[4:]:
        copy.wait()


def final_kernel(
    q_ref, k_ref, g_ref, probs_ref, a_ref, dk_ref, dv_ref, near_ref, far_ref, lq_ref,
    dq_hbm, dkc_hbm, gk_hbm, gv_hbm, lq_hbm,
    dqc_ref, dkc_ref, gk_ref, gv_ref, dp_ref, ds_ref, sems,
):
    copies = [pltpu.make_async_copy(lq_ref, lq_hbm, sems.at[0])]
    copies[0].start()

    def products(pair):
        dp_ref[pair % 2] = outer(tokens(a_ref, pair), both_heads(tokens(g_ref, pair)))

    def scores(pair):
        ds_ref[pair % 2] = score_grads(probs_ref[pair], dp_ref[pair % 2]).astype(BF16)

    def grads(pair):
        d_scores = ds_ref[pair % 2]
        queries = both_heads(tokens(q_ref, pair) * BF16(0.125))
        put(dkc_ref, pair, inner(d_scores, queries))
        grad_query = own_features(inner(tokens(k_ref, pair).T, d_scores)) * 0.125
        put(dqc_ref, pair, grad_query.astype(BF16).T)

    def sums(chunk):
        at, rows = chunk % 2, pl.ds(chunk // 2 * 8, 8)
        own, out, hbm = ((dk_ref, gk_ref, gk_hbm), (dv_ref, gv_ref, gv_hbm))[at]
        rims = near_ref[pl.ds(at, 1), rows].astype(F32) + far_ref[pl.ds(at, 1), rows].astype(F32)
        out[:, rows] = (own[:, rows] + rims).astype(BF16)
        copies.append(
            pltpu.make_async_copy(out.at[:, rows], hbm.at[:, rows], sems.at[3 + chunk])
        )
        copies[-1].start()

    def products_and_sums(pair):
        products(pair)
        sums(pair)

    pipelined(products_and_sums, scores, grads)
    for at, (out, hbm) in enumerate(((dqc_ref, dq_hbm), (dkc_ref, dkc_hbm))):
        copies.append(pltpu.make_async_copy(out, hbm, sems.at[1 + at]))
        copies[-1].start()
    for copy in copies:
        copy.wait()


def halo(near, own, far, at, pair):
    parts = (near, own.at[pl.ds(at, 1)], far.at[pl.ds(at, 1)])
    return jnp.concatenate([tokens(part, pair) for part in parts], axis=0)


def level_kernel(
    q_ref, both_ref, near_k, near_v, far_ref, g_ref, bias_ref,
    dq_ref, att_ref, dk_ref, dv_ref, near_out, far_out,
    s_ref, dp_ref, p_ref, ds_ref, qg_ref, kv_ref,
):
    bias = jnp.concatenate([bias_ref[...], bias_ref[...]], axis=1)

    def products(pair):
        queries = both_heads(tokens(q_ref, pair) * BF16(0.125))
        grads = both_heads(tokens(g_ref, pair))
        keys = halo(near_k, both_ref, far_ref, 0, pair)
        values = halo(near_v, both_ref, far_ref, 1, pair)
        s_ref[pair % 2] = outer(keys, queries) + bias
        dp_ref[pair % 2] = outer(values, grads)
        qg_ref[pair % 4, 0] = queries
        qg_ref[pair % 4, 1] = grads
        kv_ref[pair % 4, 0] = keys.T
        kv_ref[pair % 4, 1] = values.T

    def scores(pair):
        probs = softmax_over_rows(s_ref[pair % 2])
        p_ref[pair % 2] = probs.astype(BF16)
        ds_ref[pair % 2] = score_grads(probs, dp_ref[pair % 2]).astype(BF16)

    def grads(pair):
        probs_b = p_ref[pair % 2]
        d_scores = ds_ref[pair % 2]
        attended = own_features(inner(kv_ref[pair % 4, 1], probs_b))
        grad_query = own_features(inner(kv_ref[pair % 4, 0], d_scores)) * 0.125
        key_terms = inner(d_scores, qg_ref[pair % 4, 0])
        value_terms = inner(probs_b, qg_ref[pair % 4, 1])
        put(att_ref, pair, attended.astype(BF16).T)
        put(dq_ref, pair, grad_query.astype(BF16).T)
        put(near_out.at[pl.ds(0, 1)], pair, key_terms[:ROWS])
        put(near_out.at[pl.ds(1, 1)], pair, value_terms[:ROWS])
        put(dk_ref, pair, key_terms[ROWS : 2 * ROWS])
        put(dv_ref, pair, value_terms[ROWS : 2 * ROWS])
        put(far_out.at[pl.ds(0, 1)], pair, key_terms[2 * ROWS :])
        put(far_out.at[pl.ds(1, 1)], pair, value_terms[2 * ROWS :])

    pipelined(products, scores, grads)


def held(array):
    return pltpu.VMEM(array.shape, array.dtype)


def call(kernel, outs, args, units, in_specs=None, out_specs=None, scratch=()):
    moved = sum(a.size * a.dtype.itemsize for a in args)
    if in_specs is None:
        args = [pltpu.with_memory_space_constraint(a, pltpu.VMEM) for a in args]
    return pl.pallas_call(
        kernel,
        out_shape=outs,
        in_specs=in_specs or [VMEM] * len(args),
        out_specs=out_specs or [VMEM] * len(outs),
        scratch_shapes=scratch,
        cost_estimate=pl.CostEstimate(
            flops=units * 2 * ROWS * ROWS * 1024, bytes_accessed=moved, transcendentals=0
        ),
        compiler_params=pltpu.CompilerParams(vmem_limit_bytes=32 * 2**20),
    )(*args)


def on_device(
    query_level, key_level, value_level, block_lists, query_column, key_column, grad_output
):
    size = lax.axis_size("lon")
    near = [(i, i ^ 1) for i in range(size)]
    far = [(i, (i + 1) % size if i % 2 else (i - 1) % size) for i in range(size)]
    level = jax.ShapeDtypeStruct(query_level.shape, BF16)
    level32 = jax.ShapeDtypeStruct(query_level.shape, F32)
    column = jax.ShapeDtypeStruct(query_column.shape, BF16)
    two = jax.ShapeDtypeStruct((2,) + query_level.shape[1:], BF16)
    col_probs = jax.ShapeDtypeStruct((PAIRS, ROWS, 2 * ROWS), F32)
    mask = jax.ShapeDtypeStruct((3 * ROWS, ROWS), F32)
    given = [
        block_lists, query_column, key_column, grad_output, key_level, value_level, query_level,
    ]
    near_k = lax.ppermute(key_level, "lon", near)
    near_v = lax.ppermute(value_level, "lon", near)
    grad_col, both, queries, col_queries, col_keys, col_grads, probs, bias = call(
        column_forward,
        [held(a) for a in (column, two, level, column, column, column, col_probs, mask)],
        [pltpu.with_memory_space_constraint(a, pltpu.HBM) for a in given],
        4,
        in_specs=[ANY] * 7,
        scratch=[
            pltpu.SMEM(block_lists.shape, jnp.int32),
            pltpu.VMEM((2, ROWS, 2 * ROWS), F32),
            pltpu.SemaphoreType.DMA((7,)),
        ],
    )
    shared, near_k, near_v = lax.optimization_barrier((both, near_k, near_v))
    both_far = lax.ppermute(shared, "lon", far)
    grad_att = lax.all_to_all(grad_col, "lev", split_axis=0, concat_axis=1, tiled=True)
    grad_query, attended, dk, dv, near_terms, far_terms = call(
        level_kernel,
        [held(a) for a in (level, level, level32, level32, two, two)],
        [queries, both, near_k, near_v, both_far, grad_att, bias],
        18,
        scratch=[
            pltpu.VMEM((2, 3 * ROWS, 2 * ROWS), F32),
            pltpu.VMEM((2, 3 * ROWS, 2 * ROWS), F32),
            pltpu.VMEM((2, 3 * ROWS, 2 * ROWS), BF16),
            pltpu.VMEM((2, 3 * ROWS, 2 * ROWS), BF16),
            pltpu.VMEM((4, 2, 2 * ROWS, PAIR), BF16),
            pltpu.VMEM((4, 2, PAIR, 3 * ROWS), BF16),
        ],
    )
    far_sums = lax.ppermute(far_terms, "lon", far)
    near_sums = lax.ppermute(near_terms, "lon", near)
    columns = lax.all_to_all(attended, "lev", split_axis=1, concat_axis=0, tiled=True)
    grad_query_column, grad_key_column, grad_key, grad_value, grad_query = call(
        final_kernel,
        [column, column, level, level, level],
        [
            col_queries, col_keys, col_grads, probs, columns,
            dk, dv, near_sums, far_sums, grad_query,
        ],
        8,
        out_specs=[ANY] * 5,
        scratch=[pltpu.VMEM(column.shape, BF16)] * 2
        + [pltpu.VMEM(level.shape, BF16)] * 2
        + [pltpu.VMEM((2, ROWS, 2 * ROWS), F32), pltpu.VMEM((2, ROWS, 2 * ROWS), BF16)]
        + [pltpu.SemaphoreType.DMA((3 + PAIRS,))],
    )
    return grad_query, grad_key, grad_value, grad_query_column, grad_key_column


def solution(mesh):
    level = P("lev", None, "lon", None)
    column = P(None, "lev", "lon", None)
    return jax.shard_map(
        on_device,
        mesh=mesh,
        in_specs=(level, level, level, P("lon", None, None), column, column, column),
        out_specs=(level, level, level, column, column),
        check_vma=False,
    )
```

```python
import jax
import jax.numpy as jnp
from jax import lax
from jax.experimental import pallas as pl
from jax.experimental.pallas import tpu as pltpu
from jax.sharding import PartitionSpec as P

PAIRS = 8
ROWS = 128
PAIR = 128
NEGATIVE = -1e30
F32 = jnp.float32
BF16 = jnp.bfloat16

VMEM = pl.BlockSpec(memory_space=pltpu.VMEM)
ANY = pl.BlockSpec(memory_space=pl.ANY)


def tokens(ref, pair):
    return ref[:, :, :, pl.ds(pair * PAIR, PAIR)].reshape(ROWS, PAIR)


def put(ref, pair, value):
    shape = ref.shape[:-1] + (PAIR,)
    ref[:, :, :, pl.ds(pair * PAIR, PAIR)] = value.astype(ref.dtype).reshape(shape)


def both_heads(block):
    lane = lax.broadcasted_iota(jnp.int32, (1, PAIR), 1)
    first = (lane < PAIR // 2).astype(F32).astype(BF16)
    second = (lane >= PAIR // 2).astype(F32).astype(BF16)
    return jnp.concatenate([block * first, block * second], axis=0)


def outer(a, b):
    return lax.dot_general(a, b, (((1,), (1,)), ((), ())), preferred_element_type=F32)


def inner(a, b):
    return lax.dot_general(a, b, (((1,), (0,)), ((), ())), preferred_element_type=F32)


def own_features(both):
    half = PAIR // 2
    return jnp.concatenate([both[:half, :ROWS], both[half:, ROWS:]], axis=0)


def softmax_over_rows(scores):
    top = jnp.max(scores, axis=0, keepdims=True)
    raised = jnp.exp(scores - top)
    return raised * (1.0 / jnp.sum(raised, axis=0, keepdims=True))


def score_grads(probs, d_probs):
    return probs * (d_probs - jnp.sum(probs * d_probs, axis=0, keepdims=True))


def column_bias():
    key = lax.broadcasted_iota(jnp.int32, (ROWS, 2 * ROWS), 0)
    query = lax.broadcasted_iota(jnp.int32, (ROWS, 2 * ROWS), 1)
    return jnp.where((key & 15) == (query & 15), 0.0, NEGATIVE).astype(F32)


def pipelined(*stages):
    for step in range(PAIRS + len(stages) - 1):
        for delay in (0, 2, 1):
            if 0 <= step - delay < PAIRS:
                stages[delay](step - delay)


def level_bias(lists_ref):
    odd = lax.axis_index("lon") % 2
    lane = lax.broadcasted_iota(jnp.int32, (1, ROWS), 1)
    listed = jnp.zeros((1, ROWS), jnp.int32)
    for block in range(4):
        bits = jnp.int32(0)
        for j in range(15):
            bits = bits | lax.shift_left(jnp.int32(1), lists_ref[0, block, j])
        listed = jnp.where(lane // 32 == block, bits, listed)
    row = lax.broadcasted_iota(jnp.int32, (ROWS, ROWS), 0)
    block = (row // 32) * 6 + (row % 4) // 2
    parts = []
    for part in (2 - 2 * odd, 1, 2 * odd):
        allowed = lax.shift_right_logical(jnp.broadcast_to(listed, row.shape), block + 2 * part)
        parts.append(jnp.where((allowed & 1) == 1, 0.0, NEGATIVE).astype(F32))
    return jnp.concatenate(parts, axis=0)


def column_forward(
    lists_hbm, q_hbm, k_hbm, g_hbm, lk_hbm, lv_hbm, lq_hbm,
    out_ref, both_ref, lq_ref, q_ref, k_ref, g_ref, probs_ref, bias_ref,
    lists_ref, scores_ref, sems,
):
    moves = [
        (lists_hbm, lists_ref),
        (q_hbm, q_ref),
        (k_hbm, k_ref),
        (g_hbm, g_ref),
        (lk_hbm, both_ref.at[pl.ds(0, 1)]),
        (lv_hbm, both_ref.at[pl.ds(1, 1)]),
        (lq_hbm, lq_ref),
    ]
    copies = [
        pltpu.make_async_copy(src, dst, sems.at[i]) for i, (src, dst) in enumerate(moves)
    ]
    for copy in copies:
        copy.start()
    copies[0].wait()
    bias_ref[...] = level_bias(lists_ref)
    bias = column_bias()
    for copy in copies[1:4]:
        copy.wait()

    def scores(pair):
        queries = both_heads(tokens(q_ref, pair) * BF16(0.125))
        scores_ref[pair % 2] = outer(tokens(k_ref, pair), queries)

    def softmax(pair):
        probs_ref[pair] = softmax_over_rows(scores_ref[pair % 2] + bias)

    def grads(pair):
        probs = probs_ref[pair].astype(BF16)
        put(out_ref, pair, inner(probs, both_heads(tokens(g_ref, pair))))

    pipelined(scores, softmax, grads)
    for copy in copies[4:]:
        copy.wait()


def final_kernel(
    q_ref, k_ref, g_ref, probs_ref, a_ref, dk_ref, dv_ref, near_ref, far_ref, lq_ref,
    dq_hbm, dkc_hbm, gk_hbm, gv_hbm, lq_hbm,
    dqc_ref, dkc_ref, gk_ref, gv_ref, dp_ref, ds_ref, sems,
):
    copies = [pltpu.make_async_copy(lq_ref, lq_hbm, sems.at[0])]
    copies[0].start()

    def products(pair):
        dp_ref[pair % 2] = outer(tokens(a_ref, pair), both_heads(tokens(g_ref, pair)))

    def scores(pair):
        ds_ref[pair % 2] = score_grads(probs_ref[pair], dp_ref[pair % 2]).astype(BF16)

    def grads(pair):
        d_scores = ds_ref[pair % 2]
        queries = both_heads(tokens(q_ref, pair) * BF16(0.125))
        put(dkc_ref, pair, inner(d_scores, queries))
        grad_query = own_features(inner(tokens(k_ref, pair).T, d_scores)) * 0.125
        put(dqc_ref, pair, grad_query.astype(BF16).T)

    def sums(chunk):
        at, rows = chunk % 2, pl.ds(chunk // 2 * 8, 8)
        own, out, hbm = ((dk_ref, gk_ref, gk_hbm), (dv_ref, gv_ref, gv_hbm))[at]
        rims = near_ref[pl.ds(at, 1), rows].astype(F32) + far_ref[pl.ds(at, 1), rows].astype(F32)
        out[:, rows] = (own[:, rows].astype(F32) + rims).astype(BF16)
        copies.append(
            pltpu.make_async_copy(out.at[:, rows], hbm.at[:, rows], sems.at[3 + chunk])
        )
        copies[-1].start()

    def products_and_sums(pair):
        products(pair)
        sums(pair)

    pipelined(products_and_sums, scores, grads)
    for at, (out, hbm) in enumerate(((dqc_ref, dq_hbm), (dkc_ref, dkc_hbm))):
        copies.append(pltpu.make_async_copy(out, hbm, sems.at[1 + at]))
        copies[-1].start()
    for copy in copies:
        copy.wait()


def halo(near, own, far, at, pair):
    parts = (near, own.at[pl.ds(at, 1)], far.at[pl.ds(at, 1)])
    return jnp.concatenate([tokens(part, pair) for part in parts], axis=0)


def level_kernel(
    q_ref, both_ref, near_k, near_v, far_ref, g_ref, bias_ref,
    dq_ref, att_ref, dk_ref, dv_ref, near_out, far_out,
    s_ref, dp_ref, p_ref, ds_ref, qg_ref, kv_ref,
):
    bias = jnp.concatenate([bias_ref[...], bias_ref[...]], axis=1)

    def products(pair):
        queries = both_heads(tokens(q_ref, pair) * BF16(0.125))
        grads = both_heads(tokens(g_ref, pair))
        keys = halo(near_k, both_ref, far_ref, 0, pair)
        values = halo(near_v, both_ref, far_ref, 1, pair)
        s_ref[pair % 2] = outer(keys, queries) + bias
        dp_ref[pair % 2] = outer(values, grads)
        qg_ref[pair % 4, 0] = queries
        qg_ref[pair % 4, 1] = grads
        kv_ref[pair % 4, 0] = keys.T
        kv_ref[pair % 4, 1] = values.T

    def scores(pair):
        probs = softmax_over_rows(s_ref[pair % 2])
        p_ref[pair % 2] = probs.astype(BF16)
        ds_ref[pair % 2] = score_grads(probs, dp_ref[pair % 2]).astype(BF16)

    def grads(pair):
        probs_b = p_ref[pair % 2]
        d_scores = ds_ref[pair % 2]
        attended = own_features(inner(kv_ref[pair % 4, 1], probs_b))
        grad_query = own_features(inner(kv_ref[pair % 4, 0], d_scores)) * 0.125
        key_terms = inner(d_scores, qg_ref[pair % 4, 0])
        value_terms = inner(probs_b, qg_ref[pair % 4, 1])
        put(att_ref, pair, attended.astype(BF16).T)
        put(dq_ref, pair, grad_query.astype(BF16).T)
        put(near_out.at[pl.ds(0, 1)], pair, key_terms[:ROWS])
        put(near_out.at[pl.ds(1, 1)], pair, value_terms[:ROWS])
        put(dk_ref, pair, key_terms[ROWS : 2 * ROWS])
        put(dv_ref, pair, value_terms[ROWS : 2 * ROWS])
        put(far_out.at[pl.ds(0, 1)], pair, key_terms[2 * ROWS :])
        put(far_out.at[pl.ds(1, 1)], pair, value_terms[2 * ROWS :])

    pipelined(products, scores, grads)


def held(array):
    return pltpu.VMEM(array.shape, array.dtype)


def call(kernel, outs, args, units, in_specs=None, out_specs=None, scratch=()):
    moved = sum(a.size * a.dtype.itemsize for a in args)
    if in_specs is None:
        args = [pltpu.with_memory_space_constraint(a, pltpu.VMEM) for a in args]
    return pl.pallas_call(
        kernel,
        out_shape=outs,
        in_specs=in_specs or [VMEM] * len(args),
        out_specs=out_specs or [VMEM] * len(outs),
        scratch_shapes=scratch,
        cost_estimate=pl.CostEstimate(
            flops=units * 2 * ROWS * ROWS * 1024, bytes_accessed=moved, transcendentals=0
        ),
        compiler_params=pltpu.CompilerParams(vmem_limit_bytes=32 * 2**20),
    )(*args)


def on_device(
    query_level, key_level, value_level, block_lists, query_column, key_column, grad_output
):
    size = lax.axis_size("lon")
    near = [(i, i ^ 1) for i in range(size)]
    far = [(i, (i + 1) % size if i % 2 else (i - 1) % size) for i in range(size)]
    level = jax.ShapeDtypeStruct(query_level.shape, BF16)
    column = jax.ShapeDtypeStruct(query_column.shape, BF16)
    two = jax.ShapeDtypeStruct((2,) + query_level.shape[1:], BF16)
    col_probs = jax.ShapeDtypeStruct((PAIRS, ROWS, 2 * ROWS), F32)
    mask = jax.ShapeDtypeStruct((3 * ROWS, ROWS), F32)
    given = [
        block_lists, query_column, key_column, grad_output, key_level, value_level, query_level,
    ]
    near_k = lax.ppermute(key_level, "lon", near)
    near_v = lax.ppermute(value_level, "lon", near)
    grad_col, both, queries, col_queries, col_keys, col_grads, probs, bias = call(
        column_forward,
        [held(a) for a in (column, two, level, column, column, column, col_probs, mask)],
        [pltpu.with_memory_space_constraint(a, pltpu.HBM) for a in given],
        4,
        in_specs=[ANY] * 7,
        scratch=[
            pltpu.SMEM(block_lists.shape, jnp.int32),
            pltpu.VMEM((2, ROWS, 2 * ROWS), F32),
            pltpu.SemaphoreType.DMA((7,)),
        ],
    )
    shared, near_k, near_v = lax.optimization_barrier((both, near_k, near_v))
    both_far = lax.ppermute(shared, "lon", far)
    grad_att = lax.all_to_all(grad_col, "lev", split_axis=0, concat_axis=1, tiled=True)
    grad_query, attended, dk, dv, near_terms, far_terms = call(
        level_kernel,
        [held(a) for a in (level, level, level, level, two, two)],
        [queries, both, near_k, near_v, both_far, grad_att, bias],
        18,
        scratch=[
            pltpu.VMEM((2, 3 * ROWS, 2 * ROWS), F32),
            pltpu.VMEM((2, 3 * ROWS, 2 * ROWS), F32),
            pltpu.VMEM((2, 3 * ROWS, 2 * ROWS), BF16),
            pltpu.VMEM((2, 3 * ROWS, 2 * ROWS), BF16),
            pltpu.VMEM((4, 2, 2 * ROWS, PAIR), BF16),
            pltpu.VMEM((4, 2, PAIR, 3 * ROWS), BF16),
        ],
    )
    far_sums = lax.ppermute(far_terms, "lon", far)
    near_sums = lax.ppermute(near_terms, "lon", near)
    columns = lax.all_to_all(attended, "lev", split_axis=1, concat_axis=0, tiled=True)
    grad_query_column, grad_key_column, grad_key, grad_value, grad_query = call(
        final_kernel,
        [column, column, level, level, level],
        [
            col_queries, col_keys, col_grads, probs, columns,
            dk, dv, near_sums, far_sums, grad_query,
        ],
        8,
        out_specs=[ANY] * 5,
        scratch=[pltpu.VMEM(column.shape, BF16)] * 2
        + [pltpu.VMEM(level.shape, BF16)] * 2
        + [pltpu.VMEM((2, ROWS, 2 * ROWS), F32), pltpu.VMEM((2, ROWS, 2 * ROWS), BF16)]
        + [pltpu.SemaphoreType.DMA((3 + PAIRS,))],
    )
    return grad_query, grad_key, grad_value, grad_query_column, grad_key_column


def solution(mesh):
    level = P("lev", None, "lon", None)
    column = P(None, "lev", "lon", None)
    return jax.shard_map(
        on_device,
        mesh=mesh,
        in_specs=(level, level, level, P("lon", None, None), column, column, column),
        out_specs=(level, level, level, column, column),
        check_vma=False,
    )
```
